1024 devices in a mesh: expert: 64 (over x, y), tensor: 16 (over z, core).
Axes of the slice: x: 8, y: 8, z: 8, core: 2. Of those that a mesh axis runs over, the one named last changes fastest.
Arguments:
- tokens: bfloat16 [1024, 2048], P('expert', 'tensor'), may hold values from -6 to 6
- expert_ids: int32 [1024, 8], P('expert'), may hold values from 0 to 127, all different within a row; in each aligned block of 16 rows (0 to 15, 16 to 31, ...) at most 3 rows name the same one
- gate_scores: float32 [1024, 8], P('expert'), may hold values from 0.05 to 1
- w_in: bfloat16 [128, 2, 768, 2048], P('expert', None, 'tensor'), may hold values from -0.125 to 0.125
- w_down: bfloat16 [128, 768, 2048], P('expert', 'tensor'), may hold values from -0.3125 to 0.3125
Outputs:
- mixed: bfloat16 [1024, 2048], P('expert', 'tensor')
The draws below stay inside these ranges and needn't reach their ends.
Inputs may be any that keep to these rules, and one draw needn't show every extreme that they name: `expert_ids`: each row names 8 different experts; in every aligned block of 16 rows no expert is named by more than 3 rows, a bound that some block reaches.
All inputs are finite; a program needn't handle non-finite values.
Results may differ from the reference program's by a relative error of at most 0.024.
Values may be sent and summed in bfloat16 or wider, within the bound.
No kernel may reach another device: no remote copies, remote signals or barrier semaphores. Data moves between devices by JAX's collectives and lax.ppermute only.
A program may use at most 32 MiB of HBM per device.

```python
import math
import jax
import jax.numpy as jnp
import numpy as np
from jax import lax

D = 2048
FF = 768
TOP = 8
TOK_DEV = 16
EXPERTS = 128
TOKENS = 1024
CAP = 3
N_TENSOR = 16


def strengthened(drawn, key, source, target, shards_of, factor):
    owner, partner = [(jnp.arange(drawn.shape[dim]) // (drawn.shape[dim] // shards_of)).reshape([-1 if axis == dim else 1 for axis in range(drawn.ndim)]) for dim in (source, target)]
    chosen = jax.random.permutation(key, shards_of)[partner]
    strong = (owner == chosen) | (owner == (partner + shards_of // 2) % shards_of)
    return jnp.where(strong, factor * drawn, drawn)


def block_levels(own_key, shape, cuts, low, top_value):
    def one(position, blocks):
        draws = jax.random.uniform(jax.random.fold_in(jax.random.fold_in(own_key, 6), position), (blocks,), jnp.float32, low / len(cuts), top_value / len(cuts))
        return jnp.repeat(jnp.exp(draws), shape[position] // blocks).reshape((-1,) + (1,) * (len(shape) - position - 1))

    loudness = one(*cuts[0])
    for cut in cuts[1:]:
        loudness = loudness * one(*cut)
    return loudness


def deal_out(rng, own, number, rows, number_of, top, bound, skew):
    order = jax.random.permutation(rng, number_of)
    crowded, ordinary = portions_of(number_of, rows * top, bound, skew, True), portions_of(number_of, rows * top, bound, skew, False)
    places = jnp.arange(number_of)

    def named(lengths, turn):
        used = int((lengths > 0).sum())
        fixed = max(1, used // 4)
        moved = fixed + (places - fixed + turn * (used - fixed)) % max(1, number_of - fixed)
        return jnp.zeros((number_of,), jnp.int32).at[order[jnp.where(places < fixed, places, moved)]].set(jnp.asarray(lengths, jnp.int32))

    lengths = jnp.where(number % 4 == 0, named(crowded, number // 4), named(ordinary, number - number // 4 - 1))
    mixed = jax.random.permutation(jax.random.fold_in(own, 3), number_of)
    source_of, sink = mixed[0:number_of // 2 * 2:2], mixed[1:number_of // 2 * 2:2]
    room = jnp.minimum(lengths[source_of] - 1, bound - lengths[sink]) // 2
    room = jnp.where((source_of == order[0]) | (sink == order[0]) | (lengths[sink] == 0), 0, jnp.maximum(room, 0))
    moved = jax.random.randint(jax.random.fold_in(own, 4), (number_of // 2,), 0, 1 << 20) % (room + 1)
    lengths = lengths.at[source_of].add(-moved).at[sink].add(moved)
    members = jnp.searchsorted(jnp.cumsum(lengths), jnp.arange(rows * top), side="right").astype(jnp.int32)
    grid = members.reshape(top, rows).T
    grid = grid[jax.random.permutation(jax.random.fold_in(own, 1), rows)]
    turn = jax.random.randint(jax.random.fold_in(own, 2), (rows, 1), 0, top)
    return jnp.take_along_axis(grid, (jnp.arange(top)[None, :] + turn) % top, axis=1)


def portions_of(amount, total, bound, lean, full):
    portions = [(1 << 20) // math.isqrt(rank ** lean) + 1 for rank in range(1, amount + 1)]
    largest = bound if full else min(bound, max(-(-total // amount), total * portions[0] // sum(portions)))
    least = 1 if total - largest >= amount - 1 else 0
    counts, rest = [largest] + [least] * (amount - 1), total - largest - least * (amount - 1)
    while rest > 0:
        candidates = [i for i in range(1, amount) if counts[i] < largest] or [i for i in range(1, amount) if counts[i] < bound]
        mass, left = sum([portions[i] for i in candidates]), rest
        for i in candidates:
            more = min(bound - counts[i], max(1, left * portions[i] // mass), rest)
            counts[i] = counts[i] + more
            rest = rest - more
    return np.array(counts)


def gaussian(rng, extent, spread, reach, shards=(), held_as=jnp.bfloat16):
    entries = spread * jax.random.normal(rng, extent, jnp.float32)
    if shards:
        entries = entries * block_levels(rng, extent, shards, -0.22, 0.18)
    return jnp.clip(entries, -reach, reach).astype(held_as)


def bell_draw_with(key, dims, scale, reach, shards, heavy, kind=jnp.bfloat16):
    values = scale * jax.random.normal(key, dims, jnp.float32)
    if shards:
        values = values * block_levels(key, dims, shards, -0.22, 0.18)
    return jnp.clip(strengthened(values, jax.random.fold_in(key, 3), *heavy), -reach, reach).astype(kind)


def setup_inputs(seed: int = 0) -> dict:
    splits = jax.random.split(jax.random.key(seed), 6)
    tokens = gaussian(splits[0], (TOKENS, D), 1.0, 6.0, ((0, 64), (1, 16)))
    expert_ids_keys = jax.random.split(jax.random.fold_in(splits[1], 1), TOKENS // TOK_DEV)
    expert_ids_turns = jax.random.permutation(jax.random.fold_in(splits[1], 3), TOKENS // TOK_DEV)
    expert_ids = jax.vmap(lambda own, number: deal_out(jax.random.fold_in(splits[1], 2), own, number, TOK_DEV, EXPERTS, TOP, CAP, 2))(expert_ids_keys, expert_ids_turns).reshape((TOKENS, TOP))
    gate_scores = jnp.clip(jnp.exp(math.log(1.0) - 2.9957323 * jax.random.uniform(splits[2], (TOKENS, TOP), jnp.float32) ** block_levels(splits[2], (TOKENS, TOP), ((0, 64),), -0.2, 0.2)), 0.05, 1.0)
    w_in = gaussian(splits[3], (EXPERTS, 2, FF, D), D ** -0.5, 0.125, ((0, 64), (2, 16)))
    w_down = bell_draw_with(splits[4], (EXPERTS, FF, D), FF ** -0.5, 0.3125, ((0, 64), (1, 16)), (1, 2, 16, 2.0))
    return {"tokens": tokens, "expert_ids": expert_ids, "gate_scores": gate_scores, "w_in": w_in, "w_down": w_down}


def route_tables(expert_ids, gate_scores, experts, capacity):
    tok_count, top_count = expert_ids.shape
    flattened = expert_ids.reshape(tok_count * top_count)
    onehot = (flattened[:, None] == jnp.arange(experts, dtype=jnp.int32)[None, :]).astype(jnp.int32)
    before = jnp.cumsum(onehot, axis=0) - onehot
    slot_index = jnp.sum(before * onehot, axis=1)
    column = flattened * capacity + slot_index
    placing = (column[:, None] == jnp.arange(experts * capacity, dtype=jnp.int32)[None, :]).astype(jnp.float32)
    placing = placing.reshape(tok_count, top_count, experts * capacity)
    weights = gate_scores / jnp.sum(gate_scores, axis=1, keepdims=True)
    dispatch = jnp.sum(placing, axis=1)
    combine = jnp.sum(placing * weights[:, :, None], axis=1)
    return dispatch, combine


def reference(tokens, expert_ids, gate_scores, w_in, w_down):
    experts = w_in.shape[0]
    sources = TOKENS // TOK_DEV
    id_blocks = expert_ids.reshape(sources, TOK_DEV, TOP)
    score_blocks = gate_scores.reshape(sources, TOK_DEV, TOP)
    dispatch, combine = jax.vmap(lambda ids, scores: route_tables(ids, scores, experts, CAP))(id_blocks, score_blocks)
    token_blocks = tokens.reshape(sources, TOK_DEV, D)

    def gather_source(operand):
        table, block = operand
        return jnp.dot(table.T.astype(jnp.bfloat16), block, preferred_element_type=jnp.float32).astype(jnp.bfloat16)

    buffer = lax.map(gather_source, (dispatch, token_blocks))
    buffer = buffer.reshape(sources, experts, CAP, D).transpose(1, 0, 2, 3).reshape(experts, sources * CAP, D)
    group = FF // N_TENSOR

    def expert_fn(operand):
        row_block, in_rows, down_rows = operand
        count_rows = row_block.shape[0]
        preact = jnp.dot(row_block, in_rows.reshape(2 * FF, D).T, preferred_element_type=jnp.float32)
        preact = preact.reshape(count_rows, 2, FF)
        hidden = (jax.nn.silu(preact[:, 0]) * preact[:, 1]).astype(jnp.bfloat16)
        grouped = jnp.einsum("rgf,gfd->grd", hidden.reshape(count_rows, N_TENSOR, group).astype(jnp.float32),
                             down_rows.reshape(N_TENSOR, group, D).astype(jnp.float32))
        grouped = lax.optimization_barrier(grouped.astype(jnp.bfloat16)).astype(jnp.float32)
        return jnp.sum(grouped, axis=0).astype(jnp.bfloat16)

    expert_out = lax.map(expert_fn, (buffer, w_in, w_down))
    expert_out = expert_out.reshape(experts, sources, CAP, D).transpose(1, 0, 2, 3).reshape(sources, experts * CAP, D)

    def combine_source(operand):
        table, values = operand
        return jnp.dot(table, values.astype(jnp.float32), precision=lax.Precision.HIGHEST).astype(jnp.bfloat16)

    mixed = lax.map(combine_source, (combine, expert_out))
    return mixed.reshape(TOKENS, D)
```

```python
import functools

import jax
import jax.numpy as jnp
from jax import lax
from jax.experimental import pallas as pl
from jax.experimental.pallas import tpu as pltpu
from jax.sharding import PartitionSpec as P

LANES = 128
CAPACITY = 3
SPLIT = 2
VMEM = pl.BlockSpec(memory_space=pltpu.VMEM)
PARAMS = pltpu.CompilerParams(vmem_limit_bytes=48 * 1024 * 1024)


def iota(shape, dim):
    return lax.broadcasted_iota(jnp.int32, shape, dim)


def pair_column(values):
    top, toks = values.shape
    shape = (toks, top, toks)
    picked = jnp.where(iota(shape, 0) == iota(shape, 2), values[None], 0.0)
    return jnp.sum(picked, axis=2, keepdims=True)


def slot_columns(ids):
    top, toks = ids.shape
    pairs = top * toks
    down = pair_column(ids.astype(jnp.float32)).reshape(pairs, 1)
    ip, iq = iota((pairs, pairs), 0), iota((pairs, pairs), 1)
    across = jnp.sum(jnp.where(ip == iq, down, 0.0), axis=0, keepdims=True)
    same = down == across
    slot_down = jnp.sum(jnp.where(same & (iq < ip), 1.0, 0.0), axis=1, keepdims=True)
    slot_across = jnp.sum(jnp.where(same & (ip < iq), 1.0, 0.0), axis=0, keepdims=True)
    return (
        (CAPACITY * down + slot_down).astype(jnp.int32),
        (CAPACITY * across + slot_across).astype(jnp.int32),
    )


def pack_kernel(w_in_ref, w_down_ref, *out_refs):
    parts = len(out_refs)
    me = lax.axis_index("tensor")
    mine = lax.rem(me, parts)
    slices = out_refs[0].shape[1] // LANES
    hid = w_down_ref.shape[1]
    for r, out in enumerate(out_refs):
        other = jnp.bitwise_xor(mine, r)
        for j in range(slices):
            src = pl.ds(pl.multiple_of((parts * j + other) * LANES, LANES), LANES)
            dst = pl.ds(j * LANES, LANES)
            for e in range(2):
                for g in range(2):
                    out[pl.ds((2 * e + g) * hid, hid), dst] = w_in_ref[e, g, :, src]
                out[pl.ds((4 + e) * hid, hid), dst] = w_down_ref[e, :, src]


def dispatch_kernel(ids_ref, tok_ref, out_ref, scratch):
    slices, toks, _ = tok_ref.shape
    rows = out_ref.shape[0] // slices
    _, across = slot_columns(ids_ref[...])
    pairs = across.shape[1]
    placing = jnp.where(iota((rows, pairs), 0) == across, 1.0, 0.0).astype(jnp.bfloat16)
    top = pairs // toks
    token_of = jnp.where(iota((pairs, toks), 0) // top == iota((pairs, toks), 1), 1.0, 0.0)
    table = jnp.dot(
        placing, token_of.astype(jnp.bfloat16), preferred_element_type=jnp.float32
    ).astype(jnp.bfloat16)
    for j in range(slices):
        scratch[pl.ds(j, rows, stride=slices), :] = jnp.dot(
            table, tok_ref[j], preferred_element_type=jnp.float32
        )
    out_ref[...] = scratch[...].astype(jnp.bfloat16)


def unpack_rows(ref, scratch, slices):
    rows = ref.shape[0] // slices
    scratch[...] = ref[...].astype(jnp.float32)
    return jnp.concatenate(
        [
            scratch[pl.ds(j, rows, stride=slices), :].astype(jnp.bfloat16)
            for j in range(slices)
        ],
        axis=1,
    )


def first_of_pair(shape, dim):
    return lax.rem(iota(shape, dim), 2 * CAPACITY) < CAPACITY


def up_kernel(parts, *refs):
    x_ref, w_refs, out_ref, send_ref, scratch = refs[0], refs[1 : 1 + parts], *refs[1 + parts :]
    slices = w_refs[0].shape[1] // LANES
    x = unpack_rows(x_ref, scratch, slices)
    rows = x.shape[0]
    hid = w_refs[0].shape[0] // 6
    first = first_of_pair((2 * hid, rows), 1)
    for r in range(parts):
        both = lax.dot_general(
            w_refs[r][pl.ds(0, 4 * hid), :],
            x,
            (((1,), (1,)), ((), ())),
            preferred_element_type=jnp.float32,
        )
        part = jnp.where(first, both[: 2 * hid], both[2 * hid :])
        out_ref[r] = part
        send_ref[r] = part.astype(jnp.bfloat16)


def down_kernel(parts, *refs):
    own_ref, got_ref, w_refs, out_ref, scratch = (
        refs[0],
        refs[1],
        refs[2 : 2 + parts],
        *refs[2 + parts :],
    )
    slices = w_refs[0].shape[1] // LANES
    hid = w_refs[0].shape[0] // 6
    rows = own_ref.shape[2]
    first = first_of_pair((hid, rows), 1)
    values, weights = [], []
    for r in range(parts):
        pre = own_ref[r] + got_ref[r ^ 1].astype(jnp.float32)
        gate, up = pre[:hid], pre[hid:]
        hidden = gate / (1.0 + jnp.exp(-gate)) * up
        values += [jnp.where(first, hidden, 0.0), jnp.where(first, 0.0, hidden)]
        weights.append(w_refs[r][pl.ds(4 * hid, 2 * hid), :])
    values = jnp.concatenate(values, axis=0).T.astype(jnp.bfloat16)
    weights = jnp.concatenate(weights, axis=0)
    out = jnp.dot(values, weights, preferred_element_type=jnp.float32)
    for j in range(slices):
        scratch[pl.ds(j, rows, stride=slices), :] = out[:, j * LANES : (j + 1) * LANES]
    out_ref[...] = scratch[...].astype(jnp.bfloat16)


def combine_kernel(ids_ref, gates_ref, x_ref, out_ref, scratch):
    slices, toks, _ = out_ref.shape
    top = ids_ref.shape[0]
    down, _ = slot_columns(ids_ref[...])
    values = unpack_rows(x_ref, scratch, slices)
    rows = values.shape[0]
    picking = jnp.where(down == iota((top * toks, rows), 1), 1.0, 0.0).astype(jnp.bfloat16)
    picked = jnp.dot(picking, values, preferred_element_type=jnp.float32)
    gates = gates_ref[...]
    weights = pair_column(gates / jnp.sum(gates, axis=0, keepdims=True))
    mixed = jnp.sum(picked.reshape(toks, top, slices * LANES) * weights, axis=1)
    for j in range(slices):
        out_ref[j] = mixed[:, j * LANES : (j + 1) * LANES]


def call(kernel, shapes, args, scratch=()):
    return pl.pallas_call(
        kernel,
        out_shape=shapes,
        in_specs=[VMEM] * len(args),
        out_specs=jax.tree.map(lambda _: VMEM, shapes),
        scratch_shapes=list(scratch),
        compiler_params=PARAMS,
    )(*args)


def shards(tokens, expert_ids, gate_scores, w_in, w_down):
    n_expert, n_tensor = lax.axis_size("expert"), lax.axis_size("tensor")
    parts = SPLIT
    slices = n_tensor // parts
    toks = tokens.shape[0]
    exp_dev, _, hid, _ = w_in.shape
    slots = exp_dev * CAPACITY
    rows = n_expert * slots
    groups = [[parts * j + q for j in range(slices)] for q in range(parts)]
    ids, gates = expert_ids.T, gate_scores.T

    def bf16(*shape):
        return jax.ShapeDtypeStruct(shape, jnp.bfloat16)

    def f32(*shape):
        return jax.ShapeDtypeStruct(shape, jnp.float32)

    def exchange(value, r):
        return lax.ppermute(value, "tensor", [(i, i ^ r) for i in range(n_tensor)])

    packed = call(pack_kernel, [bf16(6 * hid, slices * LANES)] * parts, (w_in, w_down))
    weights = [packed[0]] + [exchange(packed[r], r) for r in range(1, parts)]

    gathered = lax.all_gather(tokens, "tensor", axis=0, axis_index_groups=groups)
    wide = pltpu.VMEM((rows * slices, LANES), jnp.float32)
    sent = call(dispatch_kernel, bf16(rows * slices, LANES), (ids, gathered), [wide])
    arrived = lax.all_to_all(
        sent.reshape(n_expert, slots * slices, LANES), "expert", 0, 0, tiled=True
    ).reshape(rows * slices, LANES)
    own, send = call(
        functools.partial(up_kernel, parts),
        [f32(parts, 2 * hid, rows), bf16(parts, 2 * hid, rows)],
        (arrived, *weights),
        [wide],
    )
    got = exchange(send, 1)
    out = call(
        functools.partial(down_kernel, parts),
        bf16(rows * slices, LANES),
        (own, got, *weights),
        [wide],
    )
    returned = lax.all_to_all(
        out.reshape(n_expert, slots * slices, LANES), "expert", 0, 0, tiled=True
    ).reshape(rows * slices, LANES)
    partial = call(combine_kernel, f32(slices, toks, LANES), (ids, gates, returned), [wide])
    pieces = lax.all_to_all(partial, "tensor", 0, 0, tiled=True, axis_index_groups=groups)
    return jnp.sum(pieces, axis=0).astype(jnp.bfloat16)


def solution(mesh):
    in_specs = (
        P("expert", "tensor"),
        P("expert", None),
        P("expert", None),
        P("expert", None, "tensor", None),
        P("expert", "tensor", None),
    )
    out_specs = P("expert", "tensor")
    return jax.shard_map(shards, mesh=mesh, in_specs=in_specs, out_specs=out_specs, check_vma=False)
```

```python
import functools

import jax
import jax.numpy as jnp
from jax import lax
from jax.experimental import pallas as pl
from jax.experimental.pallas import tpu as pltpu
from jax.sharding import PartitionSpec as P

LANES = 128
CAPACITY = 3
QUAD = 4
VMEM = pl.BlockSpec(memory_space=pltpu.VMEM)
PARAMS = pltpu.CompilerParams(vmem_limit_bytes=48 * 1024 * 1024)


def iota(shape, dim):
    return lax.broadcasted_iota(jnp.int32, shape, dim)


def pair_column(values):
    top, toks = values.shape
    shape = (toks, top, toks)
    picked = jnp.where(iota(shape, 0) == iota(shape, 2), values[None], 0.0)
    return jnp.sum(picked, axis=2, keepdims=True)


def slot_columns(ids):
    top, toks = ids.shape
    pairs = top * toks
    down = pair_column(ids.astype(jnp.float32)).reshape(pairs, 1)
    ip, iq = iota((pairs, pairs), 0), iota((pairs, pairs), 1)
    across = jnp.sum(jnp.where(ip == iq, down, 0.0), axis=0, keepdims=True)
    same = down == across
    slot_down = jnp.sum(jnp.where(same & (iq < ip), 1.0, 0.0), axis=1, keepdims=True)
    slot_across = jnp.sum(jnp.where(same & (ip < iq), 1.0, 0.0), axis=0, keepdims=True)
    return (
        (CAPACITY * down + slot_down).astype(jnp.int32),
        (CAPACITY * across + slot_across).astype(jnp.int32),
    )


def pack_kernel(w_in_ref, w_down_ref, keep_ref, core_ref, chip_ref):
    me = lax.axis_index("tensor")
    quad, place = lax.div(me, QUAD), lax.rem(me, QUAD)
    slices = keep_ref.shape[1] // LANES
    hid = w_down_ref.shape[1]
    for r, out in enumerate((keep_ref, core_ref, chip_ref.at[0], chip_ref.at[1])):
        for j in range(slices):
            owner = QUAD * jnp.bitwise_xor(quad, j) + jnp.bitwise_xor(place, r)
            src = pl.ds(pl.multiple_of(owner * LANES, LANES), LANES)
            dst = pl.ds(j * LANES, LANES)
            for e in range(2):
                for g in range(2):
                    out[pl.ds((2 * e + g) * hid, hid), dst] = w_in_ref[e, g, :, src]
                out[pl.ds((4 + e) * hid, hid), dst] = w_down_ref[e, :, src]


def dispatch_kernel(ids_ref, *refs):
    tok_refs, (out_ref, scratch) = refs[:-2], refs[-2:]
    slices = len(tok_refs)
    toks = tok_refs[0].shape[0]
    rows = out_ref.shape[0] // slices
    _, across = slot_columns(ids_ref[...])
    pairs = across.shape[1]
    placing = jnp.where(iota((rows, pairs), 0) == across, 1.0, 0.0).astype(jnp.bfloat16)
    top = pairs // toks
    token_of = jnp.where(iota((pairs, toks), 0) // top == iota((pairs, toks), 1), 1.0, 0.0)
    table = jnp.dot(
        placing, token_of.astype(jnp.bfloat16), preferred_element_type=jnp.float32
    ).astype(jnp.bfloat16)
    for j in range(slices):
        scratch[pl.ds(j, rows, stride=slices), :] = jnp.dot(
            table, tok_refs[j][...], preferred_element_type=jnp.float32
        )
    out_ref[...] = scratch[...].astype(jnp.bfloat16)


def unpack_rows(ref, scratch, slices):
    rows = ref.shape[0] // slices
    scratch[...] = ref[...].astype(jnp.float32)
    return jnp.concatenate(
        [
            scratch[pl.ds(j, rows, stride=slices), :].astype(jnp.bfloat16)
            for j in range(slices)
        ],
        axis=1,
    )


def first_of_pair(shape, dim):
    return lax.rem(iota(shape, dim), 2 * CAPACITY) < CAPACITY


def up_kernel(x_ref, w0_ref, w1_ref, w23_ref, w3_ref, own_ref, send_ref, scratch):
    slices = w0_ref.shape[1] // LANES
    x = unpack_rows(x_ref, scratch, slices)
    rows = x.shape[0]
    hid = w0_ref.shape[0] // 6
    first = first_of_pair((2 * hid, rows), 1)
    for r, w_ref in enumerate((w0_ref, w1_ref, w23_ref.at[0], w3_ref)):
        both = lax.dot_general(
            w_ref[pl.ds(0, 4 * hid), :],
            x,
            (((1,), (1,)), ((), ())),
            preferred_element_type=jnp.float32,
        )
        part = jnp.where(first, both[: 2 * hid], both[2 * hid :])
        if r % 2:
            send_ref[r // 2] = part.astype(jnp.bfloat16)
        else:
            own_ref[r // 2] = part


def add_kernel(own_ref, got_ref, sum_ref, send_ref):
    total = own_ref[...] + got_ref[...].astype(jnp.float32)
    sum_ref[...] = total
    send_ref[...] = total.astype(jnp.bfloat16)


def act_kernel(own_ref, got_ref, out_ref):
    hid = out_ref.shape[1]
    for r in range(2):
        pre = own_ref[r] + got_ref[1 - r].astype(jnp.float32)
        gate, up = pre[:hid], pre[hid:]
        out_ref[r] = (gate / (1.0 + jnp.exp(-gate)) * up).astype(jnp.bfloat16)


def down_kernel(own_ref, got_ref, w0_ref, w1_ref, w23_ref, w3_ref, out_ref, scratch):
    slices = w0_ref.shape[1] // LANES
    hid = w0_ref.shape[0] // 6
    rows = own_ref.shape[2]
    first = first_of_pair((hid, rows), 1)
    values, weights = [], []
    for r, w_ref in enumerate((w0_ref, w1_ref, w23_ref.at[0], w3_ref)):
        hidden = (got_ref if r % 2 else own_ref)[r // 2].astype(jnp.float32)
        values += [jnp.where(first, hidden, 0.0), jnp.where(first, 0.0, hidden)]
        weights.append(w_ref[pl.ds(4 * hid, 2 * hid), :])
    values = jnp.concatenate(values, axis=0).T.astype(jnp.bfloat16)
    weights = jnp.concatenate(weights, axis=0)
    out = jnp.dot(values, weights, preferred_element_type=jnp.float32)
    for j in range(slices):
        scratch[pl.ds(j, rows, stride=slices), :] = out[:, j * LANES : (j + 1) * LANES]
    out_ref[...] = scratch[...].astype(jnp.bfloat16)


def combine_kernel(ids_ref, gates_ref, x_ref, *refs):
    out_refs, scratch = refs[:-1], refs[-1]
    slices = len(out_refs)
    top, toks = ids_ref.shape
    down, _ = slot_columns(ids_ref[...])
    values = unpack_rows(x_ref, scratch, slices)
    rows = values.shape[0]
    picking = jnp.where(down == iota((top * toks, rows), 1), 1.0, 0.0).astype(jnp.bfloat16)
    picked = jnp.dot(picking, values, preferred_element_type=jnp.float32)
    gates = gates_ref[...]
    weights = pair_column(gates / jnp.sum(gates, axis=0, keepdims=True))
    mixed = jnp.sum(picked.reshape(toks, top, slices * LANES) * weights, axis=1)
    for j, out_ref in enumerate(out_refs):
        out_ref[...] = mixed[:, j * LANES : (j + 1) * LANES]


def call(kernel, shapes, args, scratch=()):
    return pl.pallas_call(
        kernel,
        out_shape=shapes,
        in_specs=[VMEM] * len(args),
        out_specs=jax.tree.map(lambda _: VMEM, shapes),
        scratch_shapes=list(scratch),
        compiler_params=PARAMS,
    )(*args)


def shards(tokens, expert_ids, gate_scores, w_in, w_down):
    n_expert, n_tensor = lax.axis_size("expert"), lax.axis_size("tensor")
    slices = n_tensor // QUAD
    toks = tokens.shape[0]
    exp_dev, _, hid, _ = w_in.shape
    slots = exp_dev * CAPACITY
    rows = n_expert * slots
    ids, gates = expert_ids.T, gate_scores.T

    def bf16(*shape):
        return jax.ShapeDtypeStruct(shape, jnp.bfloat16)

    def f32(*shape):
        return jax.ShapeDtypeStruct(shape, jnp.float32)

    def exchange(value, r):
        return lax.ppermute(value, "tensor", [(i, i ^ r) for i in range(n_tensor)])

    def across_experts(value):
        value = value.reshape(n_expert, slots * slices, LANES)
        value = lax.all_to_all(value, "expert", 0, 0, tiled=True)
        return value.reshape(rows * slices, LANES)

    gathered = [tokens] + [exchange(tokens, QUAD * r) for r in range(1, slices)]
    part = bf16(6 * hid, slices * LANES)
    keep, core, chip = call(
        pack_kernel, [part, part, bf16(2, 6 * hid, slices * LANES)], (w_in, w_down)
    )
    chip = exchange(chip, 2)
    weights = (keep, exchange(core, 1), chip, exchange(chip[1], 1))

    wide = pltpu.VMEM((rows * slices, LANES), jnp.float32)
    sent = call(dispatch_kernel, bf16(rows * slices, LANES), (ids, *gathered), [wide])
    arrived = across_experts(sent)
    pair = (2, 2 * hid, rows)
    own, send = call(up_kernel, [f32(*pair), bf16(*pair)], (arrived, *weights), [wide])
    own, send = call(add_kernel, [f32(*pair), bf16(*pair)], (own, exchange(send, 1)))
    hidden = call(act_kernel, bf16(2, hid, rows), (own, exchange(send, 2)))
    out = call(
        down_kernel, bf16(rows * slices, LANES), (hidden, exchange(hidden, 1), *weights), [wide]
    )
    returned = across_experts(out)
    mixed = call(combine_kernel, [f32(toks, LANES)] * slices, (ids, gates, returned), [wide])
    total = mixed[0]
    for r in range(1, slices):
        total = total + exchange(mixed[r], QUAD * r)
    return total.astype(jnp.bfloat16)


def solution(mesh):
    in_specs = (
        P("expert", "tensor"),
        P("expert", None),
        P("expert", None),
        P("expert", None, "tensor", None),
        P("expert", "tensor", None),
    )
    out_specs = P("expert", "tensor")
    return jax.shard_map(shards, mesh=mesh, in_specs=in_specs, out_specs=out_specs, check_vma=False)
```

```python
import jax
import jax.numpy as jnp
from jax import lax
from jax.experimental import pallas as pl
from jax.experimental.pallas import tpu as pltpu
from jax.sharding import PartitionSpec as P

LANES = 128
CAPACITY = 3
QUAD = 4
LOCAL = 2
SLOTS = LOCAL * CAPACITY
TILE = 8
VMEM = pl.BlockSpec(memory_space=pltpu.VMEM)
PARAMS = pltpu.CompilerParams(vmem_limit_bytes=48 * 1024 * 1024)


def iota(shape, dim):
    return lax.broadcasted_iota(jnp.int32, shape, dim)


def pair_column(values):
    top, toks = values.shape
    shape = (toks, top, toks)
    picked = jnp.where(iota(shape, 0) == iota(shape, 2), values[None], 0.0)
    return jnp.sum(picked, axis=2, keepdims=True)


def slot_rows(ids, owners):
    top, toks = ids.shape
    pairs = top * toks
    down = pair_column(ids.astype(jnp.float32)).reshape(pairs, 1)
    ip, iq = iota((pairs, pairs), 0), iota((pairs, pairs), 1)
    across = jnp.sum(jnp.where(ip == iq, down, 0.0), axis=0, keepdims=True)
    same = down == across
    slot_down = jnp.sum(jnp.where(same & (iq < ip), 1.0, 0.0), axis=1, keepdims=True)
    slot_across = jnp.sum(jnp.where(same & (ip < iq), 1.0, 0.0), axis=0, keepdims=True)

    def row(number, slot):
        number, slot = number.astype(jnp.int32), slot.astype(jnp.int32)
        return (number % LOCAL * CAPACITY + slot) * owners + number // LOCAL

    return row(down, slot_down), row(across, slot_across)


def rows_of(slot, group, groups, owners):
    return pl.ds(group * TILE + slot, owners, stride=groups * TILE)


def pack_kernel(w_in_ref, w_down_ref, keep_ref, core_ref, chip_ref):
    place = lax.rem(lax.axis_index("tensor"), QUAD)
    slices = keep_ref.shape[1] // LANES
    hid = w_down_ref.shape[1]
    for r, out in enumerate((keep_ref, core_ref, chip_ref.at[0], chip_ref.at[1])):
        for j in range(slices):
            owner = QUAD * j + jnp.bitwise_xor(place, r)
            src = pl.ds(pl.multiple_of(owner * LANES, LANES), LANES)
            dst = pl.ds(j * LANES, LANES)
            for e in range(LOCAL):
                for g in range(2):
                    out[pl.ds((2 * e + g) * hid, hid), dst] = w_in_ref[e, g, :, src]
                out[pl.ds((2 * LOCAL + e) * hid, hid), dst] = w_down_ref[e, :, src]


def dispatch_kernel(ids_ref, tok_ref, out_ref, scratch):
    groups = 4
    owners = out_ref.shape[0] // (groups * TILE)
    rows = owners * SLOTS
    toks = tok_ref.shape[0]
    _, across = slot_rows(ids_ref[...], owners)
    pairs = across.shape[1]
    top = pairs // toks
    placing = jnp.where(iota((rows, pairs), 0) == across, 1.0, 0.0).astype(jnp.bfloat16)
    token_of = jnp.where(iota((pairs, toks), 0) // top == iota((pairs, toks), 1), 1.0, 0.0)
    table = jnp.dot(
        placing, token_of.astype(jnp.bfloat16), preferred_element_type=jnp.float32
    ).astype(jnp.bfloat16)
    values = jnp.dot(table, tok_ref[...], preferred_element_type=jnp.float32)
    blank = jnp.zeros((owners, LANES), jnp.float32)
    for r in range(TILE):
        part = values[r * owners : (r + 1) * owners] if r < SLOTS else blank
        for m in range(groups):
            scratch[rows_of(r, m, groups, owners), :] = part
    out_ref[...] = scratch[...].astype(jnp.bfloat16)


def up_kernel(x_ref, w0_ref, w1_ref, w23_ref, w3_ref, own_ref, send_ref, scratch):
    groups = w0_ref.shape[1] // LANES
    owners = x_ref.shape[0] // (groups * TILE)
    scratch[...] = x_ref[...].astype(jnp.float32)
    x = jnp.concatenate(
        [
            jnp.concatenate(
                [scratch[rows_of(r, m, groups, owners), :] for r in range(SLOTS)], axis=0
            ).astype(jnp.bfloat16)
            for m in range(groups)
        ],
        axis=1,
    )
    rows = x.shape[0]
    hid = w0_ref.shape[0] // (3 * LOCAL)
    first = iota((2 * hid, rows), 1) < rows // LOCAL
    for r, w_ref in enumerate((w0_ref, w1_ref, w23_ref.at[0], w3_ref)):
        both = lax.dot_general(
            w_ref[pl.ds(0, 4 * hid), :],
            x,
            (((1,), (1,)), ((), ())),
            preferred_element_type=jnp.float32,
        )
        part = jnp.where(first, both[: 2 * hid], both[2 * hid :])
        if r % 2:
            send_ref[r // 2] = part.astype(jnp.bfloat16)
        else:
            own_ref[r // 2] = part


def add_kernel(own_ref, got_ref, sum_ref, send_ref):
    total = own_ref[...] + got_ref[...].astype(jnp.float32)
    sum_ref[...] = total
    send_ref[...] = total.astype(jnp.bfloat16)


def act_kernel(own_ref, got_ref, out_ref):
    hid = out_ref.shape[1]
    for r in range(2):
        pre = own_ref[r] + got_ref[1 - r].astype(jnp.float32)
        gate, up = pre[:hid], pre[hid:]
        out_ref[r] = (gate / (1.0 + jnp.exp(-gate)) * up).astype(jnp.bfloat16)


def down_kernel(own_ref, got_ref, w0_ref, w1_ref, w23_ref, w3_ref, out_ref, scratch):
    groups = w0_ref.shape[1] // LANES
    hid = w0_ref.shape[0] // (3 * LOCAL)
    rows = own_ref.shape[2]
    owners = rows // SLOTS
    first = iota((hid, rows), 1) < rows // LOCAL
    values, weights = [], []
    for r, w_ref in enumerate((w0_ref, w1_ref, w23_ref.at[0], w3_ref)):
        hidden = (got_ref if r % 2 else own_ref)[r // 2].astype(jnp.float32)
        values += [jnp.where(first, hidden, 0.0), jnp.where(first, 0.0, hidden)]
        weights.append(w_ref[pl.ds(4 * hid, 2 * hid), :])
    values = jnp.concatenate(values, axis=0).T.astype(jnp.bfloat16)
    weights = jnp.concatenate(weights, axis=0)
    out = jnp.dot(values, weights, preferred_element_type=jnp.float32)
    blank = jnp.zeros((owners, LANES), jnp.float32)
    for m in range(groups):
        for r in range(TILE):
            part = blank
            if r < SLOTS:
                part = out[r * owners : (r + 1) * owners, m * LANES : (m + 1) * LANES]
            scratch[rows_of(r, m, groups, owners), :] = part
    out_ref[...] = scratch[...].astype(jnp.bfloat16)


def combine_kernel(ids_ref, gates_ref, x_ref, out_ref, scratch):
    groups = 4
    owners = x_ref.shape[0] // (groups * TILE)
    top, toks = ids_ref.shape
    down, _ = slot_rows(ids_ref[...], owners)
    scratch[...] = x_ref[...].astype(jnp.float32)
    values = jnp.concatenate(
        [
            sum(scratch[rows_of(r, m, groups, owners), :] for m in range(groups))
            for r in range(SLOTS)
        ],
        axis=0,
    ).astype(jnp.bfloat16)
    rows = values.shape[0]
    picking = jnp.where(down == iota((top * toks, rows), 1), 1.0, 0.0).astype(jnp.bfloat16)
    picked = jnp.dot(picking, values, preferred_element_type=jnp.float32)
    gates = gates_ref[...]
    weights = pair_column(gates / jnp.sum(gates, axis=0, keepdims=True))
    mixed = jnp.sum(picked.reshape(toks, top, LANES) * weights, axis=1)
    out_ref[...] = mixed.astype(jnp.bfloat16)


def call(kernel, shapes, args, scratch=()):
    return pl.pallas_call(
        kernel,
        out_shape=shapes,
        in_specs=[VMEM] * len(args),
        out_specs=jax.tree.map(lambda _: VMEM, shapes),
        scratch_shapes=list(scratch),
        compiler_params=PARAMS,
    )(*args)


def shards(tokens, expert_ids, gate_scores, w_in, w_down):
    n_expert, n_tensor = lax.axis_size("expert"), lax.axis_size("tensor")
    groups = n_tensor // QUAD
    toks = tokens.shape[0]
    _, _, hid, _ = w_in.shape
    rows = n_expert * SLOTS
    ids, gates = expert_ids.T, gate_scores.T
    peers = [
        [e * n_tensor + QUAD * m + q for e in range(n_expert) for m in range(groups)]
        for q in range(QUAD)
    ]
    held = n_expert * groups * TILE

    def bf16(*shape):
        return jax.ShapeDtypeStruct(shape, jnp.bfloat16)

    def f32(*shape):
        return jax.ShapeDtypeStruct(shape, jnp.float32)

    def exchange(value, r):
        return lax.ppermute(value, "tensor", [(i, i ^ r) for i in range(n_tensor)])

    def deal(value):
        value = value.reshape(n_expert * groups, TILE, LANES)
        value = lax.all_to_all(
            value, ("expert", "tensor"), 0, 0, tiled=True, axis_index_groups=peers
        )
        return value.reshape(held, LANES)

    part = bf16(3 * LOCAL * hid, groups * LANES)
    keep, core, chip = call(
        pack_kernel, [part, part, bf16(2, *part.shape)], (w_in, w_down)
    )
    chip = exchange(chip, 2)
    weights = (keep, exchange(core, 1), chip, exchange(chip[1], 1))

    wide = pltpu.VMEM((held, LANES), jnp.float32)
    arrived = deal(call(dispatch_kernel, bf16(held, LANES), (ids, tokens), [wide]))
    pair = (2, 2 * hid, rows)
    own, send = call(up_kernel, [f32(*pair), bf16(*pair)], (arrived, *weights), [wide])
    own, send = call(add_kernel, [f32(*pair), bf16(*pair)], (own, exchange(send, 1)))
    hidden = call(act_kernel, bf16(2, hid, rows), (own, exchange(send, 2)))
    out = call(
        down_kernel, bf16(held, LANES), (hidden, exchange(hidden, 1), *weights), [wide]
    )
    return call(combine_kernel, bf16(toks, LANES), (ids, gates, deal(out)), [wide])


def solution(mesh):
    in_specs = (
        P("expert", "tensor"),
        P("expert", None),
        P("expert", None),
        P("expert", None, "tensor", None),
        P("expert", "tensor", None),
    )
    out_specs = P("expert", "tensor")
    return jax.shard_map(shards, mesh=mesh, in_specs=in_specs, out_specs=out_specs, check_vma=False)
```

```python
import jax
import jax.numpy as jnp
from jax import lax
from jax.experimental import pallas as pl
from jax.experimental.pallas import tpu as pltpu
from jax.sharding import PartitionSpec as P

LANES = 128
CAPACITY = 3
QUAD = 4
LOCAL = 2
SLOTS = LOCAL * CAPACITY
TILE = 8
VMEM = pl.BlockSpec(memory_space=pltpu.VMEM)
PARAMS = pltpu.CompilerParams(vmem_limit_bytes=48 * 1024 * 1024)


def iota(shape, dim):
    return lax.broadcasted_iota(jnp.int32, shape, dim)


def pair_column(values):
    top, toks = values.shape
    shape = (toks, top, toks)
    picked = jnp.where(iota(shape, 0) == iota(shape, 2), values[None], 0.0)
    return jnp.sum(picked, axis=2, keepdims=True)


def slot_rows(ids):
    top, toks = ids.shape
    pairs = top * toks
    down = pair_column(ids.astype(jnp.float32)).reshape(pairs, 1)
    ip, iq = iota((pairs, pairs), 0), iota((pairs, pairs), 1)
    across = jnp.sum(jnp.where(ip == iq, down, 0.0), axis=0, keepdims=True)
    same = down == across
    slot_down = jnp.sum(jnp.where(same & (iq < ip), 1.0, 0.0), axis=1, keepdims=True)
    slot_across = jnp.sum(jnp.where(same & (ip < iq), 1.0, 0.0), axis=0, keepdims=True)

    def row(number, slot):
        number, slot = number.astype(jnp.int32), slot.astype(jnp.int32)
        return number // LOCAL * TILE + number % LOCAL * CAPACITY + slot

    return row(down, slot_down), row(across, slot_across)


def dense_row(shape, dim, owners):
    row = iota(shape, dim)
    slot = row % TILE
    return jnp.where(slot < SLOTS, slot * owners + row // TILE, -1)


def onehot(found):
    return jnp.where(found, 1.0, 0.0).astype(jnp.bfloat16)


def pack_kernel(w_in_ref, w_down_ref, *out_refs):
    place = lax.rem(lax.axis_index("tensor"), QUAD)
    slices = out_refs[0].shape[1] // LANES
    hid = w_down_ref.shape[1]
    for r, out in enumerate(out_refs):
        for j in range(slices):
            owner = QUAD * j + jnp.bitwise_xor(place, r)
            src = pl.ds(pl.multiple_of(owner * LANES, LANES), LANES)
            dst = pl.ds(j * LANES, LANES)
            for e in range(LOCAL):
                for g in range(2):
                    out[pl.ds((2 * e + g) * hid, hid), dst] = w_in_ref[e, g, :, src]
                out[pl.ds((2 * LOCAL + e) * hid, hid), dst] = w_down_ref[e, :, src]


def dispatch_kernel(ids_ref, tok_ref, out_ref):
    owners, groups = out_ref.shape[:2]
    toks = tok_ref.shape[0]
    _, across = slot_rows(ids_ref[...])
    pairs = across.shape[1]
    token_of = onehot(iota((pairs, toks), 0) // (pairs // toks) == iota((pairs, toks), 1))
    values = jnp.dot(token_of, tok_ref[...], preferred_element_type=jnp.float32)
    placing = onehot(iota((owners * TILE, pairs), 0) == across)
    values = jnp.dot(placing, values.astype(jnp.bfloat16), preferred_element_type=jnp.float32)
    values = values.reshape(owners, TILE, LANES).astype(jnp.bfloat16)
    for m in range(groups):
        out_ref[:, m] = values


def up_kernel(x_ref, w0_ref, w1_ref, w2_ref, w3_ref, own_ref, send_ref):
    owners, groups = x_ref.shape[:2]
    held = owners * TILE
    rows = own_ref.shape[2]
    x = jnp.concatenate(
        [
            x_ref[:, m].astype(jnp.float32).reshape(held, LANES).astype(jnp.bfloat16)
            for m in range(groups)
        ],
        axis=1,
    )
    picking = onehot(iota((rows, held), 0) == dense_row((1, held), 1, owners))
    x = jnp.dot(picking, x, preferred_element_type=jnp.float32).astype(jnp.bfloat16)
    hid = w0_ref.shape[0] // (3 * LOCAL)
    first = iota((2 * hid, rows), 1) < rows // LOCAL
    for r, w_ref in enumerate((w0_ref, w1_ref, w2_ref, w3_ref)):
        both = lax.dot_general(
            w_ref[pl.ds(0, 4 * hid), :],
            x,
            (((1,), (1,)), ((), ())),
            preferred_element_type=jnp.float32,
        )
        part = jnp.where(first, both[: 2 * hid], both[2 * hid :])
        if r % 2:
            send_ref[r // 2] = part.astype(jnp.bfloat16)
        else:
            own_ref[r // 2] = part


def add_kernel(own_ref, got_ref, sum_ref, send_ref):
    total = own_ref[...] + got_ref[...].astype(jnp.float32)
    sum_ref[...] = total
    send_ref[...] = total.astype(jnp.bfloat16)


def act_kernel(own_ref, got_ref, out_ref):
    hid = out_ref.shape[1]
    for r in range(2):
        pre = own_ref[r] + got_ref[1 - r].astype(jnp.float32)
        gate, up = pre[:hid], pre[hid:]
        out_ref[r] = (gate / (1.0 + jnp.exp(-gate)) * up).astype(jnp.bfloat16)


def down_kernel(own_ref, got_ref, w0_ref, w1_ref, w2_ref, w3_ref, out_ref):
    owners, groups = out_ref.shape[:2]
    hid, rows = own_ref.shape[1:]
    first = iota((hid, rows), 1) < rows // LOCAL
    values, weights = [], []
    for r, w_ref in enumerate((w0_ref, w1_ref, w2_ref, w3_ref)):
        hidden = (got_ref if r % 2 else own_ref)[r // 2].astype(jnp.float32)
        values += [jnp.where(first, hidden, 0.0), jnp.where(first, 0.0, hidden)]
        weights.append(w_ref[pl.ds(4 * hid, 2 * hid), :])
    values = jnp.concatenate(values, axis=0).astype(jnp.bfloat16)
    weights = jnp.concatenate(weights, axis=0)
    held = owners * TILE
    placing = onehot(iota((held, rows), 1) == dense_row((held, 1), 0, owners))
    values = lax.dot_general(
        placing, values, (((1,), (1,)), ((), ())), preferred_element_type=jnp.float32
    ).astype(jnp.bfloat16)
    out = jnp.dot(values, weights, preferred_element_type=jnp.float32)
    for m in range(groups):
        part = out[:, m * LANES : (m + 1) * LANES]
        out_ref[:, m] = part.reshape(owners, TILE, LANES).astype(jnp.bfloat16)


def combine_kernel(ids_ref, gates_ref, x_ref, out_ref):
    owners, groups = x_ref.shape[:2]
    top, toks = ids_ref.shape
    held = owners * TILE
    down, _ = slot_rows(ids_ref[...])
    values = x_ref[:, 0].astype(jnp.float32)
    for m in range(1, groups):
        values = values + x_ref[:, m].astype(jnp.float32)
    values = values.reshape(held, LANES).astype(jnp.bfloat16)
    picking = onehot(down == iota((top * toks, held), 1))
    picked = jnp.dot(picking, values, preferred_element_type=jnp.float32)
    gates = gates_ref[...]
    weights = pair_column(gates / jnp.sum(gates, axis=0, keepdims=True))
    mixed = jnp.sum(picked.reshape(toks, top, LANES) * weights, axis=1)
    out_ref[...] = mixed.astype(jnp.bfloat16)


def call(kernel, shapes, args):
    return pl.pallas_call(
        kernel,
        out_shape=shapes,
        in_specs=[VMEM] * len(args),
        out_specs=jax.tree.map(lambda _: VMEM, shapes),
        compiler_params=PARAMS,
    )(*args)


def shards(tokens, expert_ids, gate_scores, w_in, w_down):
    n_expert, n_tensor = lax.axis_size("expert"), lax.axis_size("tensor")
    groups = n_tensor // QUAD
    toks = tokens.shape[0]
    _, _, hid, _ = w_in.shape
    rows = n_expert * SLOTS
    ids, gates = expert_ids.T, gate_scores.T
    peers = [
        [e * n_tensor + QUAD * m + q for e in range(n_expert) for m in range(groups)]
        for q in range(QUAD)
    ]
    held = (n_expert, groups, TILE, LANES)

    def bf16(*shape):
        return jax.ShapeDtypeStruct(shape, jnp.bfloat16)

    def f32(*shape):
        return jax.ShapeDtypeStruct(shape, jnp.float32)

    def exchange(value, r):
        return lax.ppermute(value, "tensor", [(i, i ^ r) for i in range(n_tensor)])

    def deal(value):
        value = value.reshape(n_expert * groups, TILE, LANES)
        value = lax.all_to_all(
            value, ("expert", "tensor"), 0, 0, tiled=True, axis_index_groups=peers
        )
        return value.reshape(held)

    packed = call(
        pack_kernel, [bf16(3 * LOCAL * hid, groups * LANES)] * QUAD, (w_in, w_down)
    )
    moved = {r: exchange(packed[r], r) for r in (2, 3, 1)}
    weights = [packed[0]] + [moved[r] for r in range(1, QUAD)]

    arrived = deal(call(dispatch_kernel, bf16(*held), (ids, tokens)))
    pair = (2, 2 * hid, rows)
    own, send = call(up_kernel, [f32(*pair), bf16(*pair)], (arrived, *weights))
    own, send = call(add_kernel, [f32(*pair), bf16(*pair)], (own, exchange(send, 1)))
    hidden = call(act_kernel, bf16(2, hid, rows), (own, exchange(send, 2)))
    out = call(down_kernel, bf16(*held), (hidden, exchange(hidden, 1), *weights))
    return call(combine_kernel, bf16(toks, LANES), (ids, gates, deal(out)))


def solution(mesh):
    in_specs = (
        P("expert", "tensor"),
        P("expert", None),
        P("expert", None),
        P("expert", None, "tensor", None),
        P("expert", "tensor", None),
    )
    out_specs = P("expert", "tensor")
    return jax.shard_map(shards, mesh=mesh, in_specs=in_specs, out_specs=out_specs, check_vma=False)
```

```python
import jax
import jax.numpy as jnp
from jax import lax
from jax.experimental import pallas as pl
from jax.experimental.pallas import tpu as pltpu
from jax.sharding import PartitionSpec as P

LANES = 128
CAPACITY = 3
QUAD = 4
LOCAL = 2
SLOTS = LOCAL * CAPACITY
TILE = 8
VMEM = pl.BlockSpec(memory_space=pltpu.VMEM)
MIB = 1024 * 1024


def iota(shape, dim):
    return lax.broadcasted_iota(jnp.int32, shape, dim)


def pair_column(values):
    top, toks = values.shape
    shape = (toks, top, toks)
    picked = jnp.where(iota(shape, 0) == iota(shape, 2), values[None], 0.0)
    return jnp.sum(picked, axis=2, keepdims=True)


def slot_rows(ids):
    top, toks = ids.shape
    pairs = top * toks
    down = pair_column(ids.astype(jnp.float32)).reshape(pairs, 1)
    ip, iq = iota((pairs, pairs), 0), iota((pairs, pairs), 1)
    across = jnp.sum(jnp.where(ip == iq, down, 0.0), axis=0, keepdims=True)
    same = down == across
    slot_down = jnp.sum(jnp.where(same & (iq < ip), 1.0, 0.0), axis=1, keepdims=True)
    slot_across = jnp.sum(jnp.where(same & (ip < iq), 1.0, 0.0), axis=0, keepdims=True)

    def row(number, slot):
        number, slot = number.astype(jnp.int32), slot.astype(jnp.int32)
        return number // LOCAL * TILE + number % LOCAL * CAPACITY + slot

    return row(down, slot_down), row(across, slot_across)


def dense_row(shape, dim, owners):
    row = iota(shape, dim)
    slot = row % TILE
    return jnp.where(slot < SLOTS, slot * owners + row // TILE, -1)


def onehot(found):
    return jnp.where(found, 1.0, 0.0).astype(jnp.bfloat16)


def start_kernel(
    ids_hbm,
    tok_hbm,
    w_in_hbm,
    w_down_hbm,
    sent_ref,
    keep_ref,
    core_ref,
    chip_ref,
    ids_ref,
    tok_ref,
    w_in_ref,
    w_down_ref,
    sems,
):
    moves = [(ids_hbm, ids_ref), (tok_hbm, tok_ref)]
    moves += [(w_in_hbm.at[e], w_in_ref.at[e]) for e in range(LOCAL)]
    moves += [(w_down_hbm, w_down_ref)]
    copies = [pltpu.make_async_copy(a, b, sems.at[i]) for i, (a, b) in enumerate(moves)]
    for copy in copies:
        copy.start()
    for copy in copies[:2]:
        copy.wait()

    owners, groups = sent_ref.shape[:2]
    toks = tok_ref.shape[0]
    _, across = slot_rows(ids_ref[...])
    pairs = across.shape[1]
    token_of = onehot(iota((pairs, toks), 0) // (pairs // toks) == iota((pairs, toks), 1))
    values = jnp.dot(token_of, tok_ref[...], preferred_element_type=jnp.float32)
    placing = onehot(iota((owners * TILE, pairs), 0) == across)
    values = jnp.dot(placing, values.astype(jnp.bfloat16), preferred_element_type=jnp.float32)
    values = values.reshape(owners, TILE, LANES).astype(jnp.bfloat16)
    for m in range(groups):
        sent_ref[:, m] = values

    for copy in copies[2:]:
        copy.wait()
    place = lax.rem(lax.axis_index("tensor"), QUAD)
    hid = w_down_ref.shape[1]
    for r, out in enumerate((keep_ref, core_ref, chip_ref.at[0], chip_ref.at[1])):
        for j in range(groups):
            owner = QUAD * j + jnp.bitwise_xor(place, r)
            src = pl.ds(pl.multiple_of(owner * LANES, LANES), LANES)
            dst = pl.ds(j * LANES, LANES)
            for e in range(LOCAL):
                for g in range(2):
                    out[pl.ds((2 * e + g) * hid, hid), dst] = w_in_ref[e, g, :, src]
                out[pl.ds((2 * LOCAL + e) * hid, hid), dst] = w_down_ref[e, :, src]


def up_kernel(x_ref, w0_ref, w1_ref, w2_ref, w3_ref, own_ref, send_ref):
    owners, groups = x_ref.shape[:2]
    held = owners * TILE
    rows = own_ref.shape[2]
    x = jnp.concatenate(
        [
            x_ref[:, m].astype(jnp.float32).reshape(held, LANES).astype(jnp.bfloat16)
            for m in range(groups)
        ],
        axis=1,
    )
    picking = onehot(iota((rows, held), 0) == dense_row((1, held), 1, owners))
    x = jnp.dot(picking, x, preferred_element_type=jnp.float32).astype(jnp.bfloat16)
    hid = w0_ref.shape[0] // (3 * LOCAL)
    first = iota((2 * hid, rows), 1) < rows // LOCAL
    for r, w_ref in enumerate((w0_ref, w1_ref, w2_ref.at[0], w3_ref)):
        both = lax.dot_general(
            w_ref[pl.ds(0, 4 * hid), :],
            x,
            (((1,), (1,)), ((), ())),
            preferred_element_type=jnp.float32,
        )
        part = jnp.where(first, both[: 2 * hid], both[2 * hid :])
        if r % 2:
            send_ref[r // 2] = part.astype(jnp.bfloat16)
        else:
            own_ref[r // 2] = part


def add_kernel(own_ref, got_ref, sum_ref, send_ref):
    total = own_ref[...] + got_ref[...].astype(jnp.float32)
    sum_ref[...] = total
    send_ref[...] = total.astype(jnp.bfloat16)


def act_kernel(own_ref, got_ref, out_ref):
    hid = out_ref.shape[1]
    for r in range(2):
        pre = own_ref[r] + got_ref[1 - r].astype(jnp.float32)
        gate, up = pre[:hid], pre[hid:]
        out_ref[r] = (gate / (1.0 + jnp.exp(-gate)) * up).astype(jnp.bfloat16)


def down_kernel(own_ref, got_ref, w0_ref, w1_ref, w2_ref, w3_ref, out_ref):
    owners, groups = out_ref.shape[:2]
    hid, rows = own_ref.shape[1:]
    first = iota((hid, rows), 1) < rows // LOCAL
    values, weights = [], []
    for r, w_ref in enumerate((w0_ref, w1_ref, w2_ref.at[0], w3_ref)):
        hidden = (got_ref if r % 2 else own_ref)[r // 2].astype(jnp.float32)
        values += [jnp.where(first, hidden, 0.0), jnp.where(first, 0.0, hidden)]
        weights.append(w_ref[pl.ds(4 * hid, 2 * hid), :])
    values = jnp.concatenate(values, axis=0).astype(jnp.bfloat16)
    weights = jnp.concatenate(weights, axis=0)
    held = owners * TILE
    placing = onehot(iota((held, rows), 1) == dense_row((held, 1), 0, owners))
    values = lax.dot_general(
        placing, values, (((1,), (1,)), ((), ())), preferred_element_type=jnp.float32
    ).astype(jnp.bfloat16)
    out = jnp.dot(values, weights, preferred_element_type=jnp.float32)
    for m in range(groups):
        part = out[:, m * LANES : (m + 1) * LANES]
        out_ref[:, m] = part.reshape(owners, TILE, LANES).astype(jnp.bfloat16)


def pick_kernel(ids_ref, gates_ref, picking_ref, weights_ref):
    down, _ = slot_rows(ids_ref[...])
    picking_ref[...] = onehot(down == iota(picking_ref.shape, 1))
    gates = gates_ref[...]
    weights = pair_column(gates / jnp.sum(gates, axis=0, keepdims=True))
    weights_ref[...] = jnp.broadcast_to(weights, weights_ref.shape)


def combine_kernel(picking_ref, weights_ref, x_ref, out_ref):
    owners, groups = x_ref.shape[:2]
    values = x_ref[:, 0].astype(jnp.float32)
    for m in range(1, groups):
        values = values + x_ref[:, m].astype(jnp.float32)
    values = values.reshape(owners * TILE, LANES).astype(jnp.bfloat16)
    picked = jnp.dot(picking_ref[...], values, preferred_element_type=jnp.float32)
    mixed = jnp.sum(picked.reshape(weights_ref.shape) * weights_ref[...], axis=1)
    out_ref[...] = mixed.astype(jnp.bfloat16)


def call(kernel, shapes, args, space=pltpu.VMEM, scratch=(), limit=48 * MIB):
    return pl.pallas_call(
        kernel,
        out_shape=shapes,
        in_specs=[pl.BlockSpec(memory_space=space)] * len(args),
        out_specs=jax.tree.map(lambda _: VMEM, shapes),
        scratch_shapes=list(scratch),
        compiler_params=pltpu.CompilerParams(vmem_limit_bytes=limit),
    )(*args)


def shards(tokens, expert_ids, gate_scores, w_in, w_down):
    n_expert, n_tensor = lax.axis_size("expert"), lax.axis_size("tensor")
    groups = n_tensor // QUAD
    toks = tokens.shape[0]
    _, _, hid, _ = w_in.shape
    rows = n_expert * SLOTS
    ids, gates = expert_ids.T, gate_scores.T
    peers = [
        [e * n_tensor + QUAD * m + q for e in range(n_expert) for m in range(groups)]
        for q in range(QUAD)
    ]
    held = (n_expert, groups, TILE, LANES)

    def bf16(*shape):
        return jax.ShapeDtypeStruct(shape, jnp.bfloat16)

    def f32(*shape):
        return jax.ShapeDtypeStruct(shape, jnp.float32)

    def exchange(value, r):
        return lax.ppermute(value, "tensor", [(i, i ^ r) for i in range(n_tensor)])

    def deal(value):
        value = value.reshape(n_expert * groups, TILE, LANES)
        value = lax.all_to_all(
            value, ("expert", "tensor"), 0, 0, tiled=True, axis_index_groups=peers
        )
        return value.reshape(held)

    args = (ids, tokens, w_in, w_down)
    part = bf16(3 * LOCAL * hid, groups * LANES)
    sent, keep, core, chip = call(
        start_kernel,
        [bf16(*held), part, part, bf16(2, *part.shape)],
        args,
        pl.ANY,
        [pltpu.VMEM(a.shape, a.dtype) for a in args] + [pltpu.SemaphoreType.DMA((5,))],
        60 * MIB,
    )
    chip = exchange(chip, 2)
    weights = (keep, exchange(core, 1), chip, exchange(chip[1], 1))

    pair = (2, 2 * hid, rows)
    own, send = call(up_kernel, [f32(*pair), bf16(*pair)], (deal(sent), *weights))
    own, send = call(add_kernel, [f32(*pair), bf16(*pair)], (own, exchange(send, 1)))
    hidden = call(act_kernel, bf16(2, hid, rows), (own, exchange(send, 2)))
    out = call(down_kernel, bf16(*held), (hidden, exchange(hidden, 1), *weights))

    out, ids, gates = lax.optimization_barrier((out, ids, gates))
    top = ids.shape[0]
    picking, shares = call(
        pick_kernel, [bf16(top * toks, n_expert * TILE), f32(toks, top, LANES)], (ids, gates)
    )
    return call(combine_kernel, bf16(toks, LANES), (picking, shares, deal(out)))


def solution(mesh):
    in_specs = (
        P("expert", "tensor"),
        P("expert", None),
        P("expert", None),
        P("expert", None, "tensor", None),
        P("expert", "tensor", None),
    )
    out_specs = P("expert", "tensor")
    return jax.shard_map(shards, mesh=mesh, in_specs=in_specs, out_specs=out_specs, check_vma=False)
```

```python
import jax
import jax.numpy as jnp
from jax import lax
from jax.experimental import pallas as pl
from jax.experimental.pallas import tpu as pltpu
from jax.sharding import PartitionSpec as P

LANES = 128
CAPACITY = 3
QUAD = 4
LOCAL = 2
SLOTS = LOCAL * CAPACITY
TILE = 8
VMEM = pl.BlockSpec(memory_space=pltpu.VMEM)
MIB = 1024 * 1024


def iota(shape, dim):
    return lax.broadcasted_iota(jnp.int32, shape, dim)


def pair_column(values):
    top, toks = values.shape
    shape = (toks, top, toks)
    picked = jnp.where(iota(shape, 0) == iota(shape, 2), values[None], 0.0)
    return jnp.sum(picked, axis=2, keepdims=True)


def slot_rows(ids):
    top, toks = ids.shape
    pairs = top * toks
    down = pair_column(ids.astype(jnp.float32)).reshape(pairs, 1)
    ip, iq = iota((pairs, pairs), 0), iota((pairs, pairs), 1)
    across = jnp.sum(jnp.where(ip == iq, down, 0.0), axis=0, keepdims=True)
    same = down == across
    slot_down = jnp.sum(jnp.where(same & (iq < ip), 1.0, 0.0), axis=1, keepdims=True)
    slot_across = jnp.sum(jnp.where(same & (ip < iq), 1.0, 0.0), axis=0, keepdims=True)

    def row(number, slot):
        number, slot = number.astype(jnp.int32), slot.astype(jnp.int32)
        return number // LOCAL * TILE + number % LOCAL * CAPACITY + slot

    return row(down, slot_down), row(across, slot_across)


def dense_row(shape, dim, owners):
    row = iota(shape, dim)
    slot = row % TILE
    return jnp.where(slot < SLOTS, slot * owners + row // TILE, -1)


def onehot(found):
    return jnp.where(found, 1.0, 0.0).astype(jnp.bfloat16)


def padded(values):
    owners = values.shape[0]
    blank = jnp.zeros((owners, TILE - SLOTS, LANES), values.dtype)
    return jnp.concatenate([values, blank], axis=1).reshape(owners * TILE, LANES)


def start_kernel(
    ids_hbm,
    tok_hbm,
    w_in_hbm,
    w_down_hbm,
    sent_ref,
    keep_ref,
    core_ref,
    chip_ref,
    ids_ref,
    tok_ref,
    w_in_ref,
    w_down_ref,
    sems,
):
    moves = [(ids_hbm, ids_ref), (tok_hbm, tok_ref)]
    moves += [(w_in_hbm.at[e], w_in_ref.at[e]) for e in range(LOCAL)]
    moves += [(w_down_hbm, w_down_ref)]
    copies = [pltpu.make_async_copy(a, b, sems.at[i]) for i, (a, b) in enumerate(moves)]
    for copy in copies:
        copy.start()
    for copy in copies[:2]:
        copy.wait()

    owners, groups = sent_ref.shape[:2]
    toks = tok_ref.shape[0]
    _, across = slot_rows(ids_ref[...])
    pairs = across.shape[1]
    token_of = onehot(iota((pairs, toks), 0) // (pairs // toks) == iota((pairs, toks), 1))
    values = jnp.dot(token_of, tok_ref[...], preferred_element_type=jnp.float32)
    placing = onehot(iota((owners * TILE, pairs), 0) == across)
    values = jnp.dot(placing, values.astype(jnp.bfloat16), preferred_element_type=jnp.float32)
    values = values.reshape(owners, TILE, LANES)[:, :SLOTS].astype(jnp.bfloat16)
    for m in range(groups):
        sent_ref[:, m] = values

    for copy in copies[2:]:
        copy.wait()
    place = lax.rem(lax.axis_index("tensor"), QUAD)
    hid = w_down_ref.shape[1]
    for r, out in enumerate((keep_ref, core_ref, chip_ref.at[0], chip_ref.at[1])):
        for j in range(groups):
            owner = QUAD * j + jnp.bitwise_xor(place, r)
            src = pl.ds(pl.multiple_of(owner * LANES, LANES), LANES)
            dst = pl.ds(j * LANES, LANES)
            for e in range(LOCAL):
                for g in range(2):
                    out[pl.ds((2 * e + g) * hid, hid), dst] = w_in_ref[e, g, :, src]
                out[pl.ds((2 * LOCAL + e) * hid, hid), dst] = w_down_ref[e, :, src]


def up_kernel(x_ref, w0_ref, w1_ref, w2_ref, w3_ref, own_ref, send_ref):
    owners, groups = x_ref.shape[:2]
    held = owners * TILE
    rows = own_ref.shape[2]
    x = jnp.concatenate(
        [
            padded(x_ref[:, m].astype(jnp.float32)).astype(jnp.bfloat16)
            for m in range(groups)
        ],
        axis=1,
    )
    picking = onehot(iota((rows, held), 0) == dense_row((1, held), 1, owners))
    x = jnp.dot(picking, x, preferred_element_type=jnp.float32).astype(jnp.bfloat16)
    hid = w0_ref.shape[0] // (3 * LOCAL)
    first = iota((2 * hid, rows), 1) < rows // LOCAL
    for r, w_ref in enumerate((w0_ref, w1_ref, w2_ref.at[0], w3_ref)):
        both = lax.dot_general(
            w_ref[pl.ds(0, 4 * hid), :],
            x,
            (((1,), (1,)), ((), ())),
            preferred_element_type=jnp.float32,
        )
        part = jnp.where(first, both[: 2 * hid], both[2 * hid :])
        if r % 2:
            send_ref[r // 2] = part.astype(jnp.bfloat16)
        else:
            own_ref[r // 2] = part


def add_kernel(own_ref, got_ref, sum_ref, send_ref):
    total = own_ref[...] + got_ref[...].astype(jnp.float32)
    sum_ref[...] = total
    send_ref[...] = total.astype(jnp.bfloat16)


def act_kernel(own_ref, got_ref, out_ref):
    hid = out_ref.shape[1]
    for r in range(2):
        pre = own_ref[r] + got_ref[1 - r].astype(jnp.float32)
        gate, up = pre[:hid], pre[hid:]
        out_ref[r] = (gate / (1.0 + jnp.exp(-gate)) * up).astype(jnp.bfloat16)


def down_kernel(own_ref, got_ref, w0_ref, w1_ref, w2_ref, w3_ref, out_ref):
    owners, groups = out_ref.shape[:2]
    hid, rows = own_ref.shape[1:]
    first = iota((hid, rows), 1) < rows // LOCAL
    values, weights = [], []
    for r, w_ref in enumerate((w0_ref, w1_ref, w2_ref.at[0], w3_ref)):
        hidden = (got_ref if r % 2 else own_ref)[r // 2].astype(jnp.float32)
        values += [jnp.where(first, hidden, 0.0), jnp.where(first, 0.0, hidden)]
        weights.append(w_ref[pl.ds(4 * hid, 2 * hid), :])
    values = jnp.concatenate(values, axis=0).astype(jnp.bfloat16)
    weights = jnp.concatenate(weights, axis=0)
    held = owners * TILE
    placing = onehot(iota((held, rows), 1) == dense_row((held, 1), 0, owners))
    values = lax.dot_general(
        placing, values, (((1,), (1,)), ((), ())), preferred_element_type=jnp.float32
    ).astype(jnp.bfloat16)
    out = jnp.dot(values, weights, preferred_element_type=jnp.float32)
    for m in range(groups):
        part = out[:, m * LANES : (m + 1) * LANES]
        out_ref[:, m] = part.reshape(owners, TILE, LANES)[:, :SLOTS].astype(jnp.bfloat16)


def combine_kernel(ids_ref, gates_ref, x_ref, out_ref):
    owners, groups = x_ref.shape[:2]
    top, toks = ids_ref.shape
    down, _ = slot_rows(ids_ref[...])
    values = x_ref[:, 0].astype(jnp.float32)
    for m in range(1, groups):
        values = values + x_ref[:, m].astype(jnp.float32)
    values = padded(values).astype(jnp.bfloat16)
    picking = onehot(down == iota((top * toks, owners * TILE), 1))
    picked = jnp.dot(picking, values, preferred_element_type=jnp.float32)
    gates = gates_ref[...]
    weights = pair_column(gates / jnp.sum(gates, axis=0, keepdims=True))
    mixed = jnp.sum(picked.reshape(toks, top, LANES) * weights, axis=1)
    out_ref[...] = mixed.astype(jnp.bfloat16)


def call(kernel, shapes, args, space=pltpu.VMEM, scratch=(), limit=48 * MIB):
    return pl.pallas_call(
        kernel,
        out_shape=shapes,
        in_specs=[pl.BlockSpec(memory_space=space)] * len(args),
        out_specs=jax.tree.map(lambda _: VMEM, shapes),
        scratch_shapes=list(scratch),
        compiler_params=pltpu.CompilerParams(vmem_limit_bytes=limit),
    )(*args)


def shards(tokens, expert_ids, gate_scores, w_in, w_down):
    n_expert, n_tensor = lax.axis_size("expert"), lax.axis_size("tensor")
    groups = n_tensor // QUAD
    toks = tokens.shape[0]
    _, _, hid, _ = w_in.shape
    rows = n_expert * SLOTS
    ids, gates = expert_ids.T, gate_scores.T
    peers = [
        [e * n_tensor + QUAD * m + q for e in range(n_expert) for m in range(groups)]
        for q in range(QUAD)
    ]
    held = (n_expert, groups, SLOTS, LANES)

    def bf16(*shape):
        return jax.ShapeDtypeStruct(shape, jnp.bfloat16)

    def f32(*shape):
        return jax.ShapeDtypeStruct(shape, jnp.float32)

    def exchange(value, r):
        return lax.ppermute(value, "tensor", [(i, i ^ r) for i in range(n_tensor)])

    def deal(value):
        value = value.reshape(n_expert * groups, SLOTS, LANES)
        value = lax.all_to_all(
            value, ("expert", "tensor"), 0, 0, tiled=True, axis_index_groups=peers
        )
        return value.reshape(held)

    args = (ids, tokens, w_in, w_down)
    part = bf16(3 * LOCAL * hid, groups * LANES)
    sent, keep, core, chip = call(
        start_kernel,
        [bf16(*held), part, part, bf16(2, *part.shape)],
        args,
        pl.ANY,
        [pltpu.VMEM(a.shape, a.dtype) for a in args] + [pltpu.SemaphoreType.DMA((5,))],
        60 * MIB,
    )
    chip = exchange(chip, 2)
    weights = (keep, exchange(core, 1), chip, exchange(chip[1], 1))

    pair = (2, 2 * hid, rows)
    own, send = call(up_kernel, [f32(*pair), bf16(*pair)], (deal(sent), *weights))
    own, send = call(add_kernel, [f32(*pair), bf16(*pair)], (own, exchange(send, 1)))
    hidden = call(act_kernel, bf16(2, hid, rows), (own, exchange(send, 2)))
    out = call(down_kernel, bf16(*held), (hidden, exchange(hidden, 1), *weights))
    return call(combine_kernel, bf16(toks, LANES), (ids, gates, deal(out)))


def solution(mesh):
    in_specs = (
        P("expert", "tensor"),
        P("expert", None),
        P("expert", None),
        P("expert", None, "tensor", None),
        P("expert", "tensor", None),
    )
    out_specs = P("expert", "tensor")
    return jax.shard_map(shards, mesh=mesh, in_specs=in_specs, out_specs=out_specs, check_vma=False)
```

```python
import jax
import jax.numpy as jnp
from jax import lax
from jax.experimental import pallas as pl
from jax.experimental.pallas import tpu as pltpu
from jax.sharding import PartitionSpec as P

LANES = 128
CAPACITY = 3
QUAD = 4
LOCAL = 2
SLOTS = LOCAL * CAPACITY
TILE = 8
VMEM = pl.BlockSpec(memory_space=pltpu.VMEM)
ANY = pl.BlockSpec(memory_space=pl.ANY)
MIB = 1024 * 1024


def iota(shape, dim):
    return lax.broadcasted_iota(jnp.int32, shape, dim)


def pair_column(values):
    top, toks = values.shape
    shape = (toks, top, toks)
    picked = jnp.where(iota(shape, 0) == iota(shape, 2), values[None], 0.0)
    return jnp.sum(picked, axis=2, keepdims=True)


def slot_rows(ids):
    top, toks = ids.shape
    pairs = top * toks
    down = pair_column(ids.astype(jnp.float32)).reshape(pairs, 1)
    ip, iq = iota((pairs, pairs), 0), iota((pairs, pairs), 1)
    across = jnp.sum(jnp.where(ip == iq, down, 0.0), axis=0, keepdims=True)
    same = down == across
    slot_down = jnp.sum(jnp.where(same & (iq < ip), 1.0, 0.0), axis=1, keepdims=True)
    slot_across = jnp.sum(jnp.where(same & (ip < iq), 1.0, 0.0), axis=0, keepdims=True)

    def row(number, slot):
        number, slot = number.astype(jnp.int32), slot.astype(jnp.int32)
        return number // LOCAL * TILE + number % LOCAL * CAPACITY + slot

    return row(down, slot_down), row(across, slot_across)


def dense_row(shape, dim, owners):
    row = iota(shape, dim)
    slot = row % TILE
    return jnp.where(slot < SLOTS, slot * owners + row // TILE, -1)


def onehot(found):
    return jnp.where(found, 1.0, 0.0).astype(jnp.bfloat16)


def padded(values):
    owners = values.shape[0]
    blank = jnp.zeros((owners, TILE - SLOTS, LANES), values.dtype)
    return jnp.concatenate([values, blank], axis=1).reshape(owners * TILE, LANES)


def start_kernel(
    ids_hbm, tok_hbm, w_in_hbm, w_down_hbm, sent_ref, keep_ref, core_ref, chip_ref, ids_ref, tok_ref, sems
):
    owners, groups = sent_ref.shape[:2]
    first = [
        pltpu.make_async_copy(ids_hbm, ids_ref, sems.at[0]),
        pltpu.make_async_copy(tok_hbm, tok_ref, sems.at[1]),
    ]
    for copy in first:
        copy.start()
    place = lax.rem(lax.axis_index("tensor"), QUAD)
    moves = []
    for r, out in ((2, chip_ref.at[0]), (3, chip_ref.at[1]), (1, core_ref), (0, keep_ref)):
        for j in range(groups):
            owner = QUAD * j + jnp.bitwise_xor(place, r)
            src = pl.ds(pl.multiple_of(owner * LANES, LANES), LANES)
            dst = pl.ds(j * LANES, LANES)
            for e in range(LOCAL):
                moves.append((w_in_hbm.at[e, :, :, src], out.at[pl.ds(2 * e, 2), :, dst]))
            moves.append((w_down_hbm.at[:, :, src], out.at[pl.ds(2 * LOCAL, LOCAL), :, dst]))
    rest = [pltpu.make_async_copy(a, b, sems.at[2 + i]) for i, (a, b) in enumerate(moves)]
    for copy in rest:
        copy.start()
    for copy in first:
        copy.wait()

    toks = tok_ref.shape[0]
    _, across = slot_rows(ids_ref[...])
    pairs = across.shape[1]
    token_of = onehot(iota((pairs, toks), 0) // (pairs // toks) == iota((pairs, toks), 1))
    values = jnp.dot(token_of, tok_ref[...], preferred_element_type=jnp.float32)
    placing = onehot(iota((owners * TILE, pairs), 0) == across)
    values = jnp.dot(placing, values.astype(jnp.bfloat16), preferred_element_type=jnp.float32)
    values = values.reshape(owners, TILE, LANES)[:, :SLOTS].astype(jnp.bfloat16)
    for m in range(groups):
        sent_ref[:, m] = values
    for copy in rest:
        copy.wait()


def table_kernel(ids_ref, gates_ref, dense_ref, spread_ref, picking_ref, shares_ref):
    rows, held = dense_ref.shape
    owners = held // TILE
    dense_ref[...] = onehot(iota((rows, held), 0) == dense_row((1, held), 1, owners))
    spread_ref[...] = onehot(iota((held, rows), 1) == dense_row((held, 1), 0, owners))
    down, _ = slot_rows(ids_ref[...])
    picking_ref[...] = onehot(down == iota(picking_ref.shape, 1))
    gates = gates_ref[...]
    shares = pair_column(gates / jnp.sum(gates, axis=0, keepdims=True))
    shares_ref[...] = jnp.broadcast_to(shares, shares_ref.shape)


def preact(w_ref, x):
    _, hid, depth = w_ref.shape
    rows = x.shape[0]
    both = lax.dot_general(
        w_ref[: 2 * LOCAL].reshape(2 * LOCAL * hid, depth),
        x,
        (((1,), (1,)), ((), ())),
        preferred_element_type=jnp.float32,
    )
    first = iota((2 * hid, rows), 1) < rows // LOCAL
    return jnp.where(first, both[: 2 * hid], both[2 * hid :])


def up_kernel(x_ref, dense_ref, w1_ref, w3_ref, dense_x_ref, send_ref):
    groups = x_ref.shape[1]
    x = jnp.concatenate(
        [padded(x_ref[:, m].astype(jnp.float32)).astype(jnp.bfloat16) for m in range(groups)],
        axis=1,
    )
    x = jnp.dot(dense_ref[...], x, preferred_element_type=jnp.float32).astype(jnp.bfloat16)
    dense_x_ref[...] = x
    send_ref[0] = preact(w1_ref, x).astype(jnp.bfloat16)
    send_ref[1] = preact(w3_ref, x).astype(jnp.bfloat16)


def own_kernel(x_ref, w0_ref, w2_ref, own_ref):
    x = x_ref[...]
    own_ref[0] = preact(w0_ref, x)
    own_ref[1] = preact(w2_ref.at[0], x)


def add_kernel(own_ref, got_ref, sum_ref, send_ref):
    total = own_ref[...] + got_ref[...].astype(jnp.float32)
    sum_ref[...] = total
    send_ref[...] = total.astype(jnp.bfloat16)


def act_kernel(own_ref, got_ref, out_ref):
    hid = out_ref.shape[1]
    for r in range(2):
        pre = own_ref[r] + got_ref[1 - r].astype(jnp.float32)
        gate, up = pre[:hid], pre[hid:]
        out_ref[r] = (gate / (1.0 + jnp.exp(-gate)) * up).astype(jnp.bfloat16)


def down_kernel(own_ref, got_ref, spread_ref, w0_ref, w1_ref, w2_ref, w3_ref, out_ref):
    owners, groups = out_ref.shape[:2]
    hid, rows = own_ref.shape[1:]
    first = iota((hid, rows), 1) < rows // LOCAL
    values, weights = [], []
    for r, w_ref in enumerate((w0_ref, w1_ref, w2_ref.at[0], w3_ref)):
        hidden = (got_ref if r % 2 else own_ref)[r // 2].astype(jnp.float32)
        values += [jnp.where(first, hidden, 0.0), jnp.where(first, 0.0, hidden)]
        weights.append(w_ref[2 * LOCAL :].reshape(LOCAL * hid, groups * LANES))
    values = jnp.concatenate(values, axis=0).astype(jnp.bfloat16)
    weights = jnp.concatenate(weights, axis=0)
    values = lax.dot_general(
        spread_ref[...], values, (((1,), (1,)), ((), ())), preferred_element_type=jnp.float32
    ).astype(jnp.bfloat16)
    out = jnp.dot(values, weights, preferred_element_type=jnp.float32)
    for m in range(groups):
        part = out[:, m * LANES : (m + 1) * LANES]
        out_ref[:, m] = part.reshape(owners, TILE, LANES)[:, :SLOTS].astype(jnp.bfloat16)


def combine_kernel(picking_ref, shares_ref, x_ref, out_ref):
    groups = x_ref.shape[1]
    values = x_ref[:, 0].astype(jnp.float32)
    for m in range(1, groups):
        values = values + x_ref[:, m].astype(jnp.float32)
    values = padded(values).astype(jnp.bfloat16)
    picked = jnp.dot(picking_ref[...], values, preferred_element_type=jnp.float32)
    mixed = jnp.sum(picked.reshape(shares_ref.shape) * shares_ref[...], axis=1)
    out_ref[...] = mixed.astype(jnp.bfloat16)


def call(kernel, shapes, args):
    return pl.pallas_call(
        kernel,
        out_shape=shapes,
        in_specs=[VMEM] * len(args),
        out_specs=jax.tree.map(lambda _: VMEM, shapes),
        compiler_params=pltpu.CompilerParams(vmem_limit_bytes=48 * MIB),
    )(*args)


def start(ids, tokens, w_in, w_down, sent, part):
    pair = jax.ShapeDtypeStruct((2, *part.shape), part.dtype)
    copies = 2 + 3 * QUAD * (w_in.shape[3] // (QUAD * LANES))
    return pl.pallas_call(
        start_kernel,
        out_shape=[sent, part, part, pair],
        in_specs=[ANY] * 4,
        out_specs=[VMEM, ANY, ANY, ANY],
        scratch_shapes=[
            pltpu.VMEM(ids.shape, ids.dtype),
            pltpu.VMEM(tokens.shape, tokens.dtype),
            pltpu.SemaphoreType.DMA((copies,)),
        ],
        compiler_params=pltpu.CompilerParams(vmem_limit_bytes=60 * MIB),
    )(ids, tokens, w_in, w_down)


def shards(tokens, expert_ids, gate_scores, w_in, w_down):
    n_expert, n_tensor = lax.axis_size("expert"), lax.axis_size("tensor")
    groups = n_tensor // QUAD
    toks = tokens.shape[0]
    _, _, hid, _ = w_in.shape
    rows = n_expert * SLOTS
    ids, gates = expert_ids.T, gate_scores.T
    peers = [
        [e * n_tensor + QUAD * m + q for e in range(n_expert) for m in range(groups)]
        for q in range(QUAD)
    ]
    held = (n_expert, groups, SLOTS, LANES)

    def bf16(*shape):
        return jax.ShapeDtypeStruct(shape, jnp.bfloat16)

    def f32(*shape):
        return jax.ShapeDtypeStruct(shape, jnp.float32)

    def exchange(value, r):
        return lax.ppermute(value, "tensor", [(i, i ^ r) for i in range(n_tensor)])

    def deal(value):
        value = value.reshape(n_expert * groups, SLOTS, LANES)
        value = lax.all_to_all(
            value, ("expert", "tensor"), 0, 0, tiled=True, axis_index_groups=peers
        )
        return value.reshape(held)

    part = bf16(3 * LOCAL, hid, groups * LANES)
    sent, keep, core, chip = start(ids, tokens, w_in, w_down, bf16(*held), part)
    chip, core = exchange(chip, 2), exchange(core, 1)
    weights = (keep, core, chip, exchange(chip[1], 1))

    ids, gates, core = lax.optimization_barrier((ids, gates, core))
    top, slot_table = ids.shape[0], n_expert * TILE
    dense, spread, picking, shares = call(
        table_kernel,
        [
            bf16(rows, slot_table),
            bf16(slot_table, rows),
            bf16(top * toks, slot_table),
            f32(toks, top, LANES),
        ],
        (ids, gates),
    )
    pair = (2, 2 * hid, rows)
    x, send = call(
        up_kernel,
        [bf16(rows, groups * LANES), bf16(*pair)],
        (deal(sent), dense, weights[1], weights[3]),
    )
    got = exchange(send, 1)
    own = call(own_kernel, f32(*pair), (x, weights[0], weights[2]))
    own, send = call(add_kernel, [f32(*pair), bf16(*pair)], (own, got))
    hidden = call(act_kernel, bf16(2, hid, rows), (own, exchange(send, 2)))
    out = call(down_kernel, bf16(*held), (hidden, exchange(hidden, 1), spread, *weights))
    return call(combine_kernel, bf16(toks, LANES), (picking, shares, deal(out)))


def solution(mesh):
    in_specs = (
        P("expert", "tensor"),
        P("expert", None),
        P("expert", None),
        P("expert", None, "tensor", None),
        P("expert", "tensor", None),
    )
    out_specs = P("expert", "tensor")
    return jax.shard_map(shards, mesh=mesh, in_specs=in_specs, out_specs=out_specs, check_vma=False)
```

```python
import jax
import jax.numpy as jnp
from jax import lax
from jax.experimental import pallas as pl
from jax.experimental.pallas import tpu as pltpu
from jax.sharding import PartitionSpec as P

LANES = 128
CAPACITY = 3
QUAD = 4
LOCAL = 2
SLOTS = LOCAL * CAPACITY
TILE = 8
VMEM = pl.BlockSpec(memory_space=pltpu.VMEM)
ANY = pl.BlockSpec(memory_space=pl.ANY)
MIB = 1024 * 1024


def iota(shape, dim):
    return lax.broadcasted_iota(jnp.int32, shape, dim)


def pair_column(values):
    top, toks = values.shape
    shape = (toks, top, toks)
    picked = jnp.where(iota(shape, 0) == iota(shape, 2), values[None], 0.0)
    return jnp.sum(picked, axis=2, keepdims=True)


def slot_rows(ids):
    top, toks = ids.shape
    pairs = top * toks
    down = pair_column(ids.astype(jnp.float32)).reshape(pairs, 1)
    ip, iq = iota((pairs, pairs), 0), iota((pairs, pairs), 1)
    across = jnp.sum(jnp.where(ip == iq, down, 0.0), axis=0, keepdims=True)
    same = down == across
    slot_down = jnp.sum(jnp.where(same & (iq < ip), 1.0, 0.0), axis=1, keepdims=True)
    slot_across = jnp.sum(jnp.where(same & (ip < iq), 1.0, 0.0), axis=0, keepdims=True)

    def row(number, slot):
        number, slot = number.astype(jnp.int32), slot.astype(jnp.int32)
        return number // LOCAL * TILE + number % LOCAL * CAPACITY + slot

    return row(down, slot_down), row(across, slot_across)


def dense_row(shape, dim, owners):
    row = iota(shape, dim)
    slot = row % TILE
    return jnp.where(slot < SLOTS, slot * owners + row // TILE, -1)


def onehot(found):
    return jnp.where(found, 1.0, 0.0).astype(jnp.bfloat16)


def padded(values):
    owners = values.shape[0]
    blank = jnp.zeros((owners, TILE - SLOTS, LANES), values.dtype)
    return jnp.concatenate([values, blank], axis=1).reshape(owners * TILE, LANES)


def pack(w_in_ref, w_down_ref, out_ref, distance):
    place = lax.rem(lax.axis_index("tensor"), QUAD)
    for j in range(out_ref.shape[2] // LANES):
        owner = QUAD * j + jnp.bitwise_xor(place, distance)
        src = pl.ds(pl.multiple_of(owner * LANES, LANES), LANES)
        dst = pl.ds(j * LANES, LANES)
        for e in range(LOCAL):
            for g in range(2):
                out_ref[2 * e + g, :, dst] = w_in_ref[e, g, :, src]
            out_ref[2 * LOCAL + e, :, dst] = w_down_ref[e, :, src]


def start_kernel(
    ids_hbm, tok_hbm, w_in_hbm, w_down_hbm, sent_ref, chip_ref, ids_ref, tok_ref, w_in_ref, w_down_ref, sems
):
    moves = [(ids_hbm, ids_ref), (tok_hbm, tok_ref)]
    moves += [(w_in_hbm.at[e], w_in_ref.at[e]) for e in range(LOCAL)]
    moves += [(w_down_hbm, w_down_ref)]
    copies = [pltpu.make_async_copy(a, b, sems.at[i]) for i, (a, b) in enumerate(moves)]
    for copy in copies:
        copy.start()
    for copy in copies[:2]:
        copy.wait()

    groups, owners = sent_ref.shape[:2]
    toks = tok_ref.shape[0]
    _, across = slot_rows(ids_ref[...])
    pairs = across.shape[1]
    token_of = onehot(iota((pairs, toks), 0) // (pairs // toks) == iota((pairs, toks), 1))
    values = jnp.dot(token_of, tok_ref[...], preferred_element_type=jnp.float32)
    placing = onehot(iota((owners * TILE, pairs), 0) == across)
    values = jnp.dot(placing, values.astype(jnp.bfloat16), preferred_element_type=jnp.float32)
    values = values.reshape(owners, TILE, LANES)[:, :SLOTS].astype(jnp.bfloat16)
    for m in range(groups):
        sent_ref[m] = values

    for copy in copies[2:]:
        copy.wait()
    pack(w_in_ref, w_down_ref, chip_ref.at[0], 2)
    pack(w_in_ref, w_down_ref, chip_ref.at[1], 3)


def pack_kernel(w_in_ref, w_down_ref, keep_ref, core_ref):
    pack(w_in_ref, w_down_ref, keep_ref, 0)
    pack(w_in_ref, w_down_ref, core_ref, 1)


def table_kernel(ids_ref, gates_ref, dense_ref, spread_ref, picking_ref, shares_ref):
    rows, held = dense_ref.shape
    owners = held // TILE
    dense_ref[...] = onehot(iota((rows, held), 0) == dense_row((1, held), 1, owners))
    spread_ref[...] = onehot(iota((held, rows), 1) == dense_row((held, 1), 0, owners))
    down, _ = slot_rows(ids_ref[...])
    picking_ref[...] = onehot(down == iota(picking_ref.shape, 1))
    gates = gates_ref[...]
    shares = pair_column(gates / jnp.sum(gates, axis=0, keepdims=True))
    shares_ref[...] = jnp.broadcast_to(shares, shares_ref.shape)


def preact(w_ref, x):
    _, hid, depth = w_ref.shape
    rows = x.shape[0]
    both = lax.dot_general(
        w_ref[: 2 * LOCAL].reshape(2 * LOCAL * hid, depth),
        x,
        (((1,), (1,)), ((), ())),
        preferred_element_type=jnp.float32,
    )
    first = iota((2 * hid, rows), 1) < rows // LOCAL
    return jnp.where(first, both[: 2 * hid], both[2 * hid :])


def up_kernel(x_ref, dense_ref, w1_ref, w3_ref, dense_x_ref, send_ref):
    groups = x_ref.shape[0]
    x = jnp.concatenate(
        [padded(x_ref[m].astype(jnp.float32)).astype(jnp.bfloat16) for m in range(groups)],
        axis=1,
    )
    x = jnp.dot(dense_ref[...], x, preferred_element_type=jnp.float32).astype(jnp.bfloat16)
    dense_x_ref[...] = x
    send_ref[0] = preact(w1_ref, x).astype(jnp.bfloat16)
    send_ref[1] = preact(w3_ref, x).astype(jnp.bfloat16)


def own_kernel(x_ref, w0_ref, w2_ref, own_ref):
    x = x_ref[...]
    own_ref[0] = preact(w0_ref, x)
    own_ref[1] = preact(w2_ref.at[0], x)


def add_kernel(own_ref, got_ref, sum_ref, send_ref):
    total = own_ref[...] + got_ref[...].astype(jnp.float32)
    sum_ref[...] = total
    send_ref[...] = total.astype(jnp.bfloat16)


def act_kernel(own_ref, got_ref, out_ref):
    hid = out_ref.shape[1]
    for r in range(2):
        pre = own_ref[r] + got_ref[1 - r].astype(jnp.float32)
        gate, up = pre[:hid], pre[hid:]
        out_ref[r] = (gate / (1.0 + jnp.exp(-gate)) * up).astype(jnp.bfloat16)


def down_kernel(own_ref, got_ref, spread_ref, w0_ref, w1_ref, w2_ref, w3_ref, out_ref):
    groups, owners = out_ref.shape[:2]
    hid, rows = own_ref.shape[1:]
    first = iota((hid, rows), 1) < rows // LOCAL
    values, weights = [], []
    for r, w_ref in enumerate((w0_ref, w1_ref, w2_ref.at[0], w3_ref)):
        hidden = (got_ref if r % 2 else own_ref)[r // 2].astype(jnp.float32)
        values += [jnp.where(first, hidden, 0.0), jnp.where(first, 0.0, hidden)]
        weights.append(w_ref[2 * LOCAL :].reshape(LOCAL * hid, groups * LANES))
    values = jnp.concatenate(values, axis=0).astype(jnp.bfloat16)
    weights = jnp.concatenate(weights, axis=0)
    values = lax.dot_general(
        spread_ref[...], values, (((1,), (1,)), ((), ())), preferred_element_type=jnp.float32
    ).astype(jnp.bfloat16)
    out = jnp.dot(values, weights, preferred_element_type=jnp.float32)
    for m in range(groups):
        part = out[:, m * LANES : (m + 1) * LANES]
        out_ref[m] = part.reshape(owners, TILE, LANES)[:, :SLOTS].astype(jnp.bfloat16)


def combine_kernel(picking_ref, shares_ref, x_ref, out_ref):
    groups = x_ref.shape[0]
    values = x_ref[0].astype(jnp.float32)
    for m in range(1, groups):
        values = values + x_ref[m].astype(jnp.float32)
    values = padded(values).astype(jnp.bfloat16)
    picked = jnp.dot(picking_ref[...], values, preferred_element_type=jnp.float32)
    mixed = jnp.sum(picked.reshape(shares_ref.shape) * shares_ref[...], axis=1)
    out_ref[...] = mixed.astype(jnp.bfloat16)


def call(kernel, shapes, args):
    return pl.pallas_call(
        kernel,
        out_shape=shapes,
        in_specs=[VMEM] * len(args),
        out_specs=jax.tree.map(lambda _: VMEM, shapes),
        compiler_params=pltpu.CompilerParams(vmem_limit_bytes=48 * MIB),
    )(*args)


def start(args, shapes):
    return pl.pallas_call(
        start_kernel,
        out_shape=shapes,
        in_specs=[ANY] * len(args),
        out_specs=[VMEM] * len(shapes),
        scratch_shapes=[pltpu.VMEM(a.shape, a.dtype) for a in args]
        + [pltpu.SemaphoreType.DMA((3 + LOCAL,))],
        compiler_params=pltpu.CompilerParams(vmem_limit_bytes=60 * MIB),
    )(*args)


def shards(tokens, expert_ids, gate_scores, w_in, w_down):
    n_expert, n_tensor = lax.axis_size("expert"), lax.axis_size("tensor")
    groups = n_tensor // QUAD
    toks = tokens.shape[0]
    _, _, hid, _ = w_in.shape
    rows = n_expert * SLOTS
    ids, gates = expert_ids.T, gate_scores.T
    peers = [
        [e * n_tensor + QUAD * m + q for m in range(groups) for e in range(n_expert)]
        for q in range(QUAD)
    ]
    held = (groups, n_expert, SLOTS, LANES)

    def bf16(*shape):
        return jax.ShapeDtypeStruct(shape, jnp.bfloat16)

    def f32(*shape):
        return jax.ShapeDtypeStruct(shape, jnp.float32)

    def exchange(value, r):
        return lax.ppermute(value, "tensor", [(i, i ^ r) for i in range(n_tensor)])

    def deal(value):
        value = value.reshape(n_expert * groups, SLOTS, LANES)
        value = lax.all_to_all(
            value, ("expert", "tensor"), 0, 0, tiled=True, axis_index_groups=peers
        )
        return value.reshape(held)

    part = bf16(3 * LOCAL, hid, groups * LANES)
    sent, chip = start((ids, tokens, w_in, w_down), [bf16(*held), bf16(2, *part.shape)])
    chip, w_in, w_down = lax.optimization_barrier((exchange(chip, 2), w_in, w_down))
    keep, core = call(pack_kernel, [part, part], (w_in, w_down))
    core = exchange(core, 1)
    weights = (keep, core, chip, exchange(chip[1], 1))

    ids, gates, core = lax.optimization_barrier((ids, gates, core))
    top, slot_table = ids.shape[0], n_expert * TILE
    dense, spread, picking, shares = call(
        table_kernel,
        [
            bf16(rows, slot_table),
            bf16(slot_table, rows),
            bf16(top * toks, slot_table),
            f32(toks, top, LANES),
        ],
        (ids, gates),
    )
    pair = (2, 2 * hid, rows)
    x, send = call(
        up_kernel,
        [bf16(rows, groups * LANES), bf16(*pair)],
        (deal(sent), dense, weights[1], weights[3]),
    )
    got = exchange(send, 1)
    own = call(own_kernel, f32(*pair), (x, weights[0], weights[2]))
    own, send = call(add_kernel, [f32(*pair), bf16(*pair)], (own, got))
    hidden = call(act_kernel, bf16(2, hid, rows), (own, exchange(send, 2)))
    out = call(down_kernel, bf16(*held), (hidden, exchange(hidden, 1), spread, *weights))
    return call(combine_kernel, bf16(toks, LANES), (picking, shares, deal(out)))


def solution(mesh):
    in_specs = (
        P("expert", "tensor"),
        P("expert", None),
        P("expert", None),
        P("expert", None, "tensor", None),
        P("expert", "tensor", None),
    )
    out_specs = P("expert", "tensor")
    return jax.shard_map(shards, mesh=mesh, in_specs=in_specs, out_specs=out_specs, check_vma=False)
```

```python
import jax
import jax.numpy as jnp
from jax import lax
from jax.experimental import pallas as pl
from jax.experimental.pallas import tpu as pltpu
from jax.sharding import PartitionSpec as P

LANES = 128
CAPACITY = 3
QUAD = 4
LOCAL = 2
SLOTS = LOCAL * CAPACITY
TILE = 8
VMEM = pl.BlockSpec(memory_space=pltpu.VMEM)
ANY = pl.BlockSpec(memory_space=pl.ANY)
MIB = 1024 * 1024


def iota(shape, dim):
    return lax.broadcasted_iota(jnp.int32, shape, dim)


def pair_column(values):
    top, toks = values.shape
    shape = (toks, top, toks)
    picked = jnp.where(iota(shape, 0) == iota(shape, 2), values[None], 0.0)
    return jnp.sum(picked, axis=2, keepdims=True)


def slot_rows(ids):
    top, toks = ids.shape
    pairs = top * toks
    down = pair_column(ids.astype(jnp.float32)).reshape(pairs, 1)
    ip, iq = iota((pairs, pairs), 0), iota((pairs, pairs), 1)
    across = jnp.sum(jnp.where(ip == iq, down, 0.0), axis=0, keepdims=True)
    same = down == across
    slot_down = jnp.sum(jnp.where(same & (iq < ip), 1.0, 0.0), axis=1, keepdims=True)
    slot_across = jnp.sum(jnp.where(same & (ip < iq), 1.0, 0.0), axis=0, keepdims=True)

    def row(number, slot):
        number, slot = number.astype(jnp.int32), slot.astype(jnp.int32)
        return number // LOCAL * TILE + number % LOCAL * CAPACITY + slot

    return row(down, slot_down), row(across, slot_across)


def dense_row(shape, dim, owners):
    row = iota(shape, dim)
    slot = row % TILE
    return jnp.where(slot < SLOTS, slot * owners + row // TILE, -1)


def onehot(found):
    return jnp.where(found, 1.0, 0.0).astype(jnp.bfloat16)


def padded(values):
    owners = values.shape[0]
    blank = jnp.zeros((owners, TILE - SLOTS, LANES), values.dtype)
    return jnp.concatenate([values, blank], axis=1).reshape(owners * TILE, LANES)


def pack(w_in_ref, w_down_ref, out_ref, distance):
    place = lax.rem(lax.axis_index("tensor"), QUAD)
    for j in range(out_ref.shape[2] // LANES):
        owner = QUAD * j + jnp.bitwise_xor(place, distance)
        src = pl.ds(pl.multiple_of(owner * LANES, LANES), LANES)
        dst = pl.ds(j * LANES, LANES)
        for e in range(LOCAL):
            for g in range(2):
                out_ref[2 * e + g, :, dst] = w_in_ref[e, g, :, src]
            out_ref[2 * LOCAL + e, :, dst] = w_down_ref[e, :, src]


def start_kernel(
    ids_hbm, tok_hbm, w_in_hbm, w_down_hbm, sent_ref, chip_ref, ids_ref, tok_ref, w_in_ref, w_down_ref, sems
):
    moves = [(ids_hbm, ids_ref), (tok_hbm, tok_ref)]
    moves += [(w_in_hbm.at[e], w_in_ref.at[e]) for e in range(LOCAL)]
    moves += [(w_down_hbm, w_down_ref)]
    copies = [pltpu.make_async_copy(a, b, sems.at[i]) for i, (a, b) in enumerate(moves)]
    for copy in copies:
        copy.start()
    for copy in copies[:2]:
        copy.wait()

    owners, groups = sent_ref.shape[:2]
    toks = tok_ref.shape[0]
    _, across = slot_rows(ids_ref[...])
    pairs = across.shape[1]
    token_of = onehot(iota((pairs, toks), 0) // (pairs // toks) == iota((pairs, toks), 1))
    values = jnp.dot(token_of, tok_ref[...], preferred_element_type=jnp.float32)
    placing = onehot(iota((owners * TILE, pairs), 0) == across)
    values = jnp.dot(placing, values.astype(jnp.bfloat16), preferred_element_type=jnp.float32)
    values = values.reshape(owners, TILE, LANES)[:, :SLOTS].astype(jnp.bfloat16)
    for m in range(groups):
        sent_ref[:, m] = values

    for copy in copies[2:]:
        copy.wait()
    pack(w_in_ref, w_down_ref, chip_ref.at[0], 2)
    pack(w_in_ref, w_down_ref, chip_ref.at[1], 3)


def pack_kernel(w_in_ref, w_down_ref, keep_ref, core_ref):
    pack(w_in_ref, w_down_ref, keep_ref, 0)
    pack(w_in_ref, w_down_ref, core_ref, 1)


def table_kernel(ids_ref, gates_ref, dense_ref, spread_ref, picking_ref, shares_ref):
    rows, held = dense_ref.shape
    owners = held // TILE
    dense_ref[...] = onehot(iota((rows, held), 0) == dense_row((1, held), 1, owners))
    spread_ref[...] = onehot(iota((held, rows), 1) == dense_row((held, 1), 0, owners))
    down, _ = slot_rows(ids_ref[...])
    picking_ref[...] = onehot(down == iota(picking_ref.shape, 1))
    gates = gates_ref[...]
    shares = pair_column(gates / jnp.sum(gates, axis=0, keepdims=True))
    shares_ref[...] = jnp.broadcast_to(shares, shares_ref.shape)


def preact(w_ref, x):
    _, hid, depth = w_ref.shape
    rows = x.shape[0]
    both = lax.dot_general(
        w_ref[: 2 * LOCAL].reshape(2 * LOCAL * hid, depth),
        x,
        (((1,), (1,)), ((), ())),
        preferred_element_type=jnp.float32,
    )
    first = iota((2 * hid, rows), 1) < rows // LOCAL
    return jnp.where(first, both[: 2 * hid], both[2 * hid :])


def up_kernel(x_ref, dense_ref, w1_ref, w3_ref, dense_x_ref, send_ref):
    groups = x_ref.shape[1]
    x = jnp.concatenate(
        [padded(x_ref[:, m].astype(jnp.float32)).astype(jnp.bfloat16) for m in range(groups)],
        axis=1,
    )
    x = jnp.dot(dense_ref[...], x, preferred_element_type=jnp.float32).astype(jnp.bfloat16)
    dense_x_ref[...] = x
    send_ref[0] = preact(w1_ref, x).astype(jnp.bfloat16)
    send_ref[1] = preact(w3_ref, x).astype(jnp.bfloat16)


def own_kernel(x_ref, w0_ref, w2_ref, own_ref):
    x = x_ref[...]
    own_ref[0] = preact(w0_ref, x)
    own_ref[1] = preact(w2_ref.at[0], x)


def add_kernel(own_ref, got_ref, sum_ref, send_ref):
    total = own_ref[...] + got_ref[...].astype(jnp.float32)
    sum_ref[...] = total
    send_ref[...] = total.astype(jnp.bfloat16)


def act_kernel(own_ref, got_ref, out_ref):
    hid = out_ref.shape[1]
    for r in range(2):
        pre = own_ref[r] + got_ref[1 - r].astype(jnp.float32)
        gate, up = pre[:hid], pre[hid:]
        out_ref[r] = (gate / (1.0 + jnp.exp(-gate)) * up).astype(jnp.bfloat16)


def down_kernel(own_ref, got_ref, spread_ref, w0_ref, w1_ref, w2_ref, w3_ref, out_ref):
    owners, groups = out_ref.shape[:2]
    hid, rows = own_ref.shape[1:]
    first = iota((hid, rows), 1) < rows // LOCAL
    values, weights = [], []
    for r, w_ref in enumerate((w0_ref, w1_ref, w2_ref.at[0], w3_ref)):
        hidden = (got_ref if r % 2 else own_ref)[r // 2].astype(jnp.float32)
        values += [jnp.where(first, hidden, 0.0), jnp.where(first, 0.0, hidden)]
        weights.append(w_ref[2 * LOCAL :].reshape(LOCAL * hid, groups * LANES))
    values = jnp.concatenate(values, axis=0).astype(jnp.bfloat16)
    weights = jnp.concatenate(weights, axis=0)
    values = lax.dot_general(
        spread_ref[...], values, (((1,), (1,)), ((), ())), preferred_element_type=jnp.float32
    ).astype(jnp.bfloat16)
    out = jnp.dot(values, weights, preferred_element_type=jnp.float32)
    for m in range(groups):
        part = out[:, m * LANES : (m + 1) * LANES]
        out_ref[:, m] = part.reshape(owners, TILE, LANES)[:, :SLOTS].astype(jnp.bfloat16)


def combine_kernel(picking_ref, shares_ref, x_ref, out_ref):
    groups = x_ref.shape[1]
    values = x_ref[:, 0].astype(jnp.float32)
    for m in range(1, groups):
        values = values + x_ref[:, m].astype(jnp.float32)
    values = padded(values).astype(jnp.bfloat16)
    picked = jnp.dot(picking_ref[...], values, preferred_element_type=jnp.float32)
    mixed = jnp.sum(picked.reshape(shares_ref.shape) * shares_ref[...], axis=1)
    out_ref[...] = mixed.astype(jnp.bfloat16)


def call(kernel, shapes, args):
    return pl.pallas_call(
        kernel,
        out_shape=shapes,
        in_specs=[VMEM] * len(args),
        out_specs=jax.tree.map(lambda _: VMEM, shapes),
        compiler_params=pltpu.CompilerParams(vmem_limit_bytes=48 * MIB),
    )(*args)


def start(args, shapes):
    return pl.pallas_call(
        start_kernel,
        out_shape=shapes,
        in_specs=[ANY] * len(args),
        out_specs=[VMEM] * len(shapes),
        scratch_shapes=[pltpu.VMEM(a.shape, a.dtype) for a in args]
        + [pltpu.SemaphoreType.DMA((3 + LOCAL,))],
        compiler_params=pltpu.CompilerParams(vmem_limit_bytes=60 * MIB),
    )(*args)


def shards(tokens, expert_ids, gate_scores, w_in, w_down):
    n_expert, n_tensor = lax.axis_size("expert"), lax.axis_size("tensor")
    groups = n_tensor // QUAD
    toks = tokens.shape[0]
    _, _, hid, _ = w_in.shape
    rows = n_expert * SLOTS
    ids, gates = expert_ids.T, gate_scores.T
    peers = [
        [e * n_tensor + QUAD * m + q for e in range(n_expert) for m in range(groups)]
        for q in range(QUAD)
    ]
    held = (n_expert, groups, SLOTS, LANES)

    def bf16(*shape):
        return jax.ShapeDtypeStruct(shape, jnp.bfloat16)

    def f32(*shape):
        return jax.ShapeDtypeStruct(shape, jnp.float32)

    def exchange(value, r):
        return lax.ppermute(value, "tensor", [(i, i ^ r) for i in range(n_tensor)])

    def deal(value):
        value = value.reshape(n_expert * groups, SLOTS, LANES)
        value = lax.all_to_all(
            value, ("expert", "tensor"), 0, 0, tiled=True, axis_index_groups=peers
        )
        return value.reshape(held)

    part = bf16(3 * LOCAL, hid, groups * LANES)
    sent, chip = start((ids, tokens, w_in, w_down), [bf16(*held), bf16(2, *part.shape)])
    chip, w_in, w_down = lax.optimization_barrier((exchange(chip, 2), w_in, w_down))
    keep, core = call(pack_kernel, [part, part], (w_in, w_down))
    core = exchange(core, 1)
    weights = (keep, core, chip, exchange(chip[1], 1))

    ids, gates, core = lax.optimization_barrier((ids, gates, core))
    top, slot_table = ids.shape[0], n_expert * TILE
    dense, spread, picking, shares = call(
        table_kernel,
        [
            bf16(rows, slot_table),
            bf16(slot_table, rows),
            bf16(top * toks, slot_table),
            f32(toks, top, LANES),
        ],
        (ids, gates),
    )
    pair = (2, 2 * hid, rows)
    x, send = call(
        up_kernel,
        [bf16(rows, groups * LANES), bf16(*pair)],
        (deal(sent), dense, weights[1], weights[3]),
    )
    got = exchange(send, 1)
    own = call(own_kernel, f32(*pair), (x, weights[0], weights[2]))
    own, send = call(add_kernel, [f32(*pair), bf16(*pair)], (own, got))
    hidden = call(act_kernel, bf16(2, hid, rows), (own, exchange(send, 2)))
    out = call(down_kernel, bf16(*held), (hidden, exchange(hidden, 1), spread, *weights))
    return call(combine_kernel, bf16(toks, LANES), (picking, shares, deal(out)))


def solution(mesh):
    in_specs = (
        P("expert", "tensor"),
        P("expert", None),
        P("expert", None),
        P("expert", None, "tensor", None),
        P("expert", "tensor", None),
    )
    out_specs = P("expert", "tensor")
    return jax.shard_map(shards, mesh=mesh, in_specs=in_specs, out_specs=out_specs, check_vma=False)
```

```python
import jax
import jax.numpy as jnp
from jax import lax
from jax.experimental import pallas as pl
from jax.experimental.pallas import tpu as pltpu
from jax.sharding import PartitionSpec as P

LANES = 128
CAPACITY = 3
QUAD = 4
LOCAL = 2
SLOTS = LOCAL * CAPACITY
TILE = 8
VMEM = pl.BlockSpec(memory_space=pltpu.VMEM)
ANY = pl.BlockSpec(memory_space=pl.ANY)
MIB = 1024 * 1024


def iota(shape, dim):
    return lax.broadcasted_iota(jnp.int32, shape, dim)


def pair_column(values):
    top, toks = values.shape
    shape = (toks, top, toks)
    picked = jnp.where(iota(shape, 0) == iota(shape, 2), values[None], 0.0)
    return jnp.sum(picked, axis=2, keepdims=True)


def slot_rows(ids):
    top, toks = ids.shape
    pairs = top * toks
    down = pair_column(ids.astype(jnp.float32)).reshape(pairs, 1)
    ip, iq = iota((pairs, pairs), 0), iota((pairs, pairs), 1)
    across = jnp.sum(jnp.where(ip == iq, down, 0.0), axis=0, keepdims=True)
    same = down == across
    slot_down = jnp.sum(jnp.where(same & (iq < ip), 1.0, 0.0), axis=1, keepdims=True)
    slot_across = jnp.sum(jnp.where(same & (ip < iq), 1.0, 0.0), axis=0, keepdims=True)

    def row(number, slot):
        number, slot = number.astype(jnp.int32), slot.astype(jnp.int32)
        return number // LOCAL * TILE + number % LOCAL * CAPACITY + slot

    return row(down, slot_down), row(across, slot_across)


def dense_row(shape, dim, owners):
    row = iota(shape, dim)
    slot = row % TILE
    return jnp.where(slot < SLOTS, slot * owners + row // TILE, -1)


def onehot(found):
    return jnp.where(found, 1.0, 0.0).astype(jnp.bfloat16)


def padded(values):
    owners = values.shape[0]
    blank = jnp.zeros((owners, TILE - SLOTS, LANES), values.dtype)
    return jnp.concatenate([values, blank], axis=1).reshape(owners * TILE, LANES)


def start_kernel(ids_hbm, tok_hbm, sent_ref, ids_ref, tok_ref, sems):
    copies = [
        pltpu.make_async_copy(ids_hbm, ids_ref, sems.at[0]),
        pltpu.make_async_copy(tok_hbm, tok_ref, sems.at[1]),
    ]
    for copy in copies:
        copy.start()
    for copy in copies:
        copy.wait()
    owners, groups = sent_ref.shape[:2]
    toks = tok_ref.shape[0]
    _, across = slot_rows(ids_ref[...])
    pairs = across.shape[1]
    token_of = onehot(iota((pairs, toks), 0) // (pairs // toks) == iota((pairs, toks), 1))
    values = jnp.dot(token_of, tok_ref[...], preferred_element_type=jnp.float32)
    placing = onehot(iota((owners * TILE, pairs), 0) == across)
    values = jnp.dot(placing, values.astype(jnp.bfloat16), preferred_element_type=jnp.float32)
    values = values.reshape(owners, TILE, LANES)[:, :SLOTS].astype(jnp.bfloat16)
    for m in range(groups):
        sent_ref[:, m] = values


def pack_kernel(w_in_ref, w_down_ref, keep_ref, core_ref, up2_ref, up3_ref, down2_ref, down3_ref):
    place = lax.rem(lax.axis_index("tensor"), QUAD)
    both = 2 * LOCAL
    ups = (keep_ref, core_ref, up2_ref, up3_ref)
    downs = (keep_ref.at[both:], core_ref.at[both:], down2_ref, down3_ref)
    for r in range(QUAD):
        for j in range(keep_ref.shape[2] // LANES):
            owner = QUAD * j + jnp.bitwise_xor(place, r)
            src = pl.ds(pl.multiple_of(owner * LANES, LANES), LANES)
            dst = pl.ds(j * LANES, LANES)
            for e in range(LOCAL):
                for g in range(2):
                    ups[r][2 * e + g, :, dst] = w_in_ref[e, g, :, src]
                downs[r][e, :, dst] = w_down_ref[e, :, src]


def table_kernel(ids_ref, gates_ref, dense_ref, spread_ref, picking_ref, shares_ref):
    rows, held = dense_ref.shape
    owners = held // TILE
    dense_ref[...] = onehot(iota((rows, held), 0) == dense_row((1, held), 1, owners))
    spread_ref[...] = onehot(iota((held, rows), 1) == dense_row((held, 1), 0, owners))
    down, _ = slot_rows(ids_ref[...])
    picking_ref[...] = onehot(down == iota(picking_ref.shape, 1))
    gates = gates_ref[...]
    shares = pair_column(gates / jnp.sum(gates, axis=0, keepdims=True))
    shares_ref[...] = jnp.broadcast_to(shares, shares_ref.shape)


def preact(w_ref, x):
    _, hid, depth = w_ref.shape
    rows = x.shape[0]
    both = lax.dot_general(
        w_ref[: 2 * LOCAL].reshape(2 * LOCAL * hid, depth),
        x,
        (((1,), (1,)), ((), ())),
        preferred_element_type=jnp.float32,
    )
    first = iota((2 * hid, rows), 1) < rows // LOCAL
    return jnp.where(first, both[: 2 * hid], both[2 * hid :])


def up_kernel(x_ref, dense_ref, w1_ref, w3_ref, dense_x_ref, send_ref):
    groups = x_ref.shape[1]
    x = jnp.concatenate(
        [padded(x_ref[:, m].astype(jnp.float32)).astype(jnp.bfloat16) for m in range(groups)],
        axis=1,
    )
    x = jnp.dot(dense_ref[...], x, preferred_element_type=jnp.float32).astype(jnp.bfloat16)
    dense_x_ref[...] = x
    send_ref[0] = preact(w1_ref, x).astype(jnp.bfloat16)
    send_ref[1] = preact(w3_ref, x).astype(jnp.bfloat16)


def own_kernel(x_ref, w0_ref, w2_ref, own_ref):
    x = x_ref[...]
    own_ref[0] = preact(w0_ref, x)
    own_ref[1] = preact(w2_ref, x)


def add_kernel(own_ref, got_ref, sum_ref, send_ref):
    total = own_ref[...] + got_ref[...].astype(jnp.float32)
    sum_ref[...] = total
    send_ref[...] = total.astype(jnp.bfloat16)


def act_kernel(own_ref, got_ref, out_ref):
    hid = out_ref.shape[1]
    for r in range(2):
        pre = own_ref[r] + got_ref[1 - r].astype(jnp.float32)
        gate, up = pre[:hid], pre[hid:]
        out_ref[r] = (gate / (1.0 + jnp.exp(-gate)) * up).astype(jnp.bfloat16)


def down_kernel(own_ref, got_ref, spread_ref, w0_ref, w1_ref, w2_ref, w3_ref, out_ref):
    owners, groups = out_ref.shape[:2]
    hid, rows = own_ref.shape[1:]
    first = iota((hid, rows), 1) < rows // LOCAL
    values, weights = [], []
    both = 2 * LOCAL
    for r, w_ref in enumerate((w0_ref.at[both:], w1_ref.at[both:], w2_ref, w3_ref)):
        hidden = (got_ref if r % 2 else own_ref)[r // 2].astype(jnp.float32)
        values += [jnp.where(first, hidden, 0.0), jnp.where(first, 0.0, hidden)]
        weights.append(w_ref[...].reshape(LOCAL * hid, groups * LANES))
    values = jnp.concatenate(values, axis=0).astype(jnp.bfloat16)
    weights = jnp.concatenate(weights, axis=0)
    values = lax.dot_general(
        spread_ref[...], values, (((1,), (1,)), ((), ())), preferred_element_type=jnp.float32
    ).astype(jnp.bfloat16)
    out = jnp.dot(values, weights, preferred_element_type=jnp.float32)
    for m in range(groups):
        part = out[:, m * LANES : (m + 1) * LANES]
        out_ref[:, m] = part.reshape(owners, TILE, LANES)[:, :SLOTS].astype(jnp.bfloat16)


def combine_kernel(picking_ref, shares_ref, x_ref, out_ref):
    groups = x_ref.shape[1]
    values = x_ref[:, 0].astype(jnp.float32)
    for m in range(1, groups):
        values = values + x_ref[:, m].astype(jnp.float32)
    values = padded(values).astype(jnp.bfloat16)
    picked = jnp.dot(picking_ref[...], values, preferred_element_type=jnp.float32)
    mixed = jnp.sum(picked.reshape(shares_ref.shape) * shares_ref[...], axis=1)
    out_ref[...] = mixed.astype(jnp.bfloat16)


def call(kernel, shapes, args):
    return pl.pallas_call(
        kernel,
        out_shape=shapes,
        in_specs=[VMEM] * len(args),
        out_specs=jax.tree.map(lambda _: VMEM, shapes),
        compiler_params=pltpu.CompilerParams(vmem_limit_bytes=48 * MIB),
    )(*args)


def start(args, shape):
    return pl.pallas_call(
        start_kernel,
        out_shape=shape,
        in_specs=[ANY] * len(args),
        out_specs=VMEM,
        scratch_shapes=[pltpu.VMEM(a.shape, a.dtype) for a in args]
        + [pltpu.SemaphoreType.DMA((len(args),))],
        compiler_params=pltpu.CompilerParams(vmem_limit_bytes=60 * MIB),
    )(*args)


def shards(tokens, expert_ids, gate_scores, w_in, w_down):
    n_expert, n_tensor = lax.axis_size("expert"), lax.axis_size("tensor")
    groups = n_tensor // QUAD
    toks = tokens.shape[0]
    _, _, hid, _ = w_in.shape
    rows = n_expert * SLOTS
    ids, gates = expert_ids.T, gate_scores.T
    peers = [
        [e * n_tensor + QUAD * m + q for e in range(n_expert) for m in range(groups)]
        for q in range(QUAD)
    ]
    held = (n_expert, groups, SLOTS, LANES)

    def bf16(*shape):
        return jax.ShapeDtypeStruct(shape, jnp.bfloat16)

    def f32(*shape):
        return jax.ShapeDtypeStruct(shape, jnp.float32)

    def exchange(value, r):
        return lax.ppermute(value, "tensor", [(i, i ^ r) for i in range(n_tensor)])

    def deal(value):
        value = value.reshape(n_expert * groups, SLOTS, LANES)
        value = lax.all_to_all(
            value, ("expert", "tensor"), 0, 0, tiled=True, axis_index_groups=peers
        )
        return value.reshape(held)

    sent = start((ids, tokens), bf16(*held))
    part, wide, deep = [bf16(n * LOCAL, hid, groups * LANES) for n in (3, 2, 1)]
    keep, core, up2, up3, down2, down3 = call(
        pack_kernel, [part, part, wide, wide, deep, deep], (w_in, w_down)
    )
    up2, up3, core = exchange(up2, 2), exchange(up3, 3), exchange(core, 1)
    up2, up3, down2, down3 = lax.optimization_barrier((up2, up3, down2, down3))
    down2, down3 = exchange(down2, 2), exchange(down3, 3)

    ids, gates, core = lax.optimization_barrier((ids, gates, core))
    top, slot_table = ids.shape[0], n_expert * TILE
    dense, spread, picking, shares = call(
        table_kernel,
        [
            bf16(rows, slot_table),
            bf16(slot_table, rows),
            bf16(top * toks, slot_table),
            f32(toks, top, LANES),
        ],
        (ids, gates),
    )
    pair = (2, 2 * hid, rows)
    x, send = call(
        up_kernel,
        [bf16(rows, groups * LANES), bf16(*pair)],
        (deal(sent), dense, core, up3),
    )
    got = exchange(send, 1)
    own = call(own_kernel, f32(*pair), (x, keep, up2))
    own, send = call(add_kernel, [f32(*pair), bf16(*pair)], (own, got))
    hidden = call(act_kernel, bf16(2, hid, rows), (own, exchange(send, 2)))
    out = call(down_kernel, bf16(*held), (hidden, exchange(hidden, 1), spread, keep, core, down2, down3))
    return call(combine_kernel, bf16(toks, LANES), (picking, shares, deal(out)))


def solution(mesh):
    in_specs = (
        P("expert", "tensor"),
        P("expert", None),
        P("expert", None),
        P("expert", None, "tensor", None),
        P("expert", "tensor", None),
    )
    out_specs = P("expert", "tensor")
    return jax.shard_map(shards, mesh=mesh, in_specs=in_specs, out_specs=out_specs, check_vma=False)
```

```python
import functools

import jax
import jax.numpy as jnp
from jax import lax
from jax.experimental import pallas as pl
from jax.experimental.pallas import tpu as pltpu
from jax.sharding import PartitionSpec as P

LANES = 128
CAPACITY = 3
QUAD = 4
LOCAL = 2
SLOTS = LOCAL * CAPACITY
TILE = 8
VMEM = pl.BlockSpec(memory_space=pltpu.VMEM)
ANY = pl.BlockSpec(memory_space=pl.ANY)
MIB = 1024 * 1024


def iota(shape, dim):
    return lax.broadcasted_iota(jnp.int32, shape, dim)


def pair_column(values):
    top, toks = values.shape
    shape = (toks, top, toks)
    picked = jnp.where(iota(shape, 0) == iota(shape, 2), values[None], 0.0)
    return jnp.sum(picked, axis=2, keepdims=True)


def slot_rows(ids):
    top, toks = ids.shape
    pairs = top * toks
    down = pair_column(ids.astype(jnp.float32)).reshape(pairs, 1)
    ip, iq = iota((pairs, pairs), 0), iota((pairs, pairs), 1)
    across = jnp.sum(jnp.where(ip == iq, down, 0.0), axis=0, keepdims=True)
    same = down == across
    slot_down = jnp.sum(jnp.where(same & (iq < ip), 1.0, 0.0), axis=1, keepdims=True)
    slot_across = jnp.sum(jnp.where(same & (ip < iq), 1.0, 0.0), axis=0, keepdims=True)

    def row(number, slot):
        number, slot = number.astype(jnp.int32), slot.astype(jnp.int32)
        return number // LOCAL * TILE + number % LOCAL * CAPACITY + slot

    return row(down, slot_down), row(across, slot_across)


def dense_row(shape, dim, owners):
    row = iota(shape, dim)
    slot = row % TILE
    return jnp.where(slot < SLOTS, slot * owners + row // TILE, -1)


def onehot(found):
    return jnp.where(found, 1.0, 0.0).astype(jnp.bfloat16)


def padded(values):
    owners = values.shape[0]
    blank = jnp.zeros((owners, TILE - SLOTS, LANES), values.dtype)
    return jnp.concatenate([values, blank], axis=1).reshape(owners * TILE, LANES)


def pack(w_in_ref, w_down_ref, out_ref, distance):
    place = lax.rem(lax.axis_index("tensor"), QUAD)
    for j in range(out_ref.shape[2] // LANES):
        owner = QUAD * j + jnp.bitwise_xor(place, distance)
        src = pl.ds(pl.multiple_of(owner * LANES, LANES), LANES)
        dst = pl.ds(j * LANES, LANES)
        for e in range(LOCAL):
            for g in range(2):
                out_ref[2 * e + g, :, dst] = w_in_ref[e, g, :, src]
            out_ref[2 * LOCAL + e, :, dst] = w_down_ref[e, :, src]


def start_kernel(
    ids_hbm, tok_hbm, w_in_hbm, w_down_hbm, sent_ref, chip_ref, ids_ref, tok_ref, w_in_ref, w_down_ref, sems
):
    moves = [(ids_hbm, ids_ref), (tok_hbm, tok_ref)]
    moves += [(w_in_hbm.at[e], w_in_ref.at[e]) for e in range(LOCAL)]
    moves += [(w_down_hbm, w_down_ref)]
    copies = [pltpu.make_async_copy(a, b, sems.at[i]) for i, (a, b) in enumerate(moves)]
    for copy in copies:
        copy.start()
    for copy in copies[:2]:
        copy.wait()

    owners, groups = sent_ref.shape[:2]
    toks = tok_ref.shape[0]
    _, across = slot_rows(ids_ref[...])
    pairs = across.shape[1]
    token_of = onehot(iota((pairs, toks), 0) // (pairs // toks) == iota((pairs, toks), 1))
    values = jnp.dot(token_of, tok_ref[...], preferred_element_type=jnp.float32)
    placing = onehot(iota((owners * TILE, pairs), 0) == across)
    values = jnp.dot(placing, values.astype(jnp.bfloat16), preferred_element_type=jnp.float32)
    values = values.reshape(owners, TILE, LANES)[:, :SLOTS].astype(jnp.bfloat16)
    for m in range(groups):
        sent_ref[:, m] = values

    for copy in copies[2:]:
        copy.wait()
    pack(w_in_ref, w_down_ref, chip_ref.at[0], 2)
    pack(w_in_ref, w_down_ref, chip_ref.at[1], 3)


def pack_kernel(w_in_ref, w_down_ref, keep_ref, core_ref):
    pack(w_in_ref, w_down_ref, keep_ref, 0)
    pack(w_in_ref, w_down_ref, core_ref, 1)


def table_kernel(ids_ref, gates_ref, dense_ref, spread_ref, picking_ref, shares_ref):
    rows, held = dense_ref.shape
    owners = held // TILE
    dense_ref[...] = onehot(iota((rows, held), 0) == dense_row((1, held), 1, owners))
    spread_ref[...] = onehot(iota((held, rows), 1) == dense_row((held, 1), 0, owners))
    down, _ = slot_rows(ids_ref[...])
    picking_ref[...] = onehot(down == iota(picking_ref.shape, 1))
    gates = gates_ref[...]
    shares = pair_column(gates / jnp.sum(gates, axis=0, keepdims=True))
    shares_ref[...] = jnp.broadcast_to(shares, shares_ref.shape)


def preact(w_ref, x):
    _, hid, depth = w_ref.shape
    rows = x.shape[0]
    both = lax.dot_general(
        w_ref[: 2 * LOCAL].reshape(2 * LOCAL * hid, depth),
        x,
        (((1,), (1,)), ((), ())),
        preferred_element_type=jnp.float32,
    )
    first = iota((2 * hid, rows), 1) < rows // LOCAL
    return jnp.where(first, both[: 2 * hid], both[2 * hid :])


def up_kernel(x_ref, dense_ref, w1_ref, w3_ref, dense_x_ref, send_ref):
    groups = x_ref.shape[1]
    x = jnp.concatenate(
        [padded(x_ref[:, m].astype(jnp.float32)).astype(jnp.bfloat16) for m in range(groups)],
        axis=1,
    )
    x = jnp.dot(dense_ref[...], x, preferred_element_type=jnp.float32).astype(jnp.bfloat16)
    dense_x_ref[...] = x
    send_ref[0] = preact(w1_ref, x).astype(jnp.bfloat16)
    send_ref[1] = preact(w3_ref, x).astype(jnp.bfloat16)


def own_kernel(x_ref, w0_ref, w2_ref, own_ref):
    x = x_ref[...]
    own_ref[0] = preact(w0_ref, x)
    own_ref[1] = preact(w2_ref.at[0], x)


def add_kernel(own_ref, got_ref, sum_ref, send0_ref, send2_ref):
    total = own_ref[...] + got_ref[...].astype(jnp.float32)
    sum_ref[...] = total
    send0_ref[...] = total[0].astype(jnp.bfloat16)
    send2_ref[...] = total[1].astype(jnp.bfloat16)


def act_kernel(block, own_ref, got_ref, out_ref):
    hid = out_ref.shape[0]
    pre = own_ref[block] + got_ref[...].astype(jnp.float32)
    gate, up = pre[:hid], pre[hid:]
    out_ref[...] = (gate / (1.0 + jnp.exp(-gate)) * up).astype(jnp.bfloat16)


def down_kernel(
    h0_ref, h1_ref, h2_ref, h3_ref, spread_ref, w0_ref, w1_ref, w2_ref, w3_ref, out_ref
):
    owners, groups = out_ref.shape[:2]
    hid, rows = h0_ref.shape
    first = iota((hid, rows), 1) < rows // LOCAL
    values, weights = [], []
    for h_ref, w_ref in (
        (h0_ref, w0_ref),
        (h1_ref, w1_ref),
        (h2_ref, w2_ref.at[0]),
        (h3_ref, w3_ref),
    ):
        hidden = h_ref[...].astype(jnp.float32)
        values += [jnp.where(first, hidden, 0.0), jnp.where(first, 0.0, hidden)]
        weights.append(w_ref[2 * LOCAL :].reshape(LOCAL * hid, groups * LANES))
    values = jnp.concatenate(values, axis=0).astype(jnp.bfloat16)
    weights = jnp.concatenate(weights, axis=0)
    values = lax.dot_general(
        spread_ref[...], values, (((1,), (1,)), ((), ())), preferred_element_type=jnp.float32
    ).astype(jnp.bfloat16)
    out = jnp.dot(values, weights, preferred_element_type=jnp.float32)
    for m in range(groups):
        part = out[:, m * LANES : (m + 1) * LANES]
        out_ref[:, m] = part.reshape(owners, TILE, LANES)[:, :SLOTS].astype(jnp.bfloat16)


def combine_kernel(picking_ref, shares_ref, x_ref, out_ref):
    groups = x_ref.shape[1]
    values = x_ref[:, 0].astype(jnp.float32)
    for m in range(1, groups):
        values = values + x_ref[:, m].astype(jnp.float32)
    values = padded(values).astype(jnp.bfloat16)
    picked = jnp.dot(picking_ref[...], values, preferred_element_type=jnp.float32)
    mixed = jnp.sum(picked.reshape(shares_ref.shape) * shares_ref[...], axis=1)
    out_ref[...] = mixed.astype(jnp.bfloat16)


def call(kernel, shapes, args):
    return pl.pallas_call(
        kernel,
        out_shape=shapes,
        in_specs=[VMEM] * len(args),
        out_specs=jax.tree.map(lambda _: VMEM, shapes),
        compiler_params=pltpu.CompilerParams(vmem_limit_bytes=48 * MIB),
    )(*args)


def start(args, shapes):
    return pl.pallas_call(
        start_kernel,
        out_shape=shapes,
        in_specs=[ANY] * len(args),
        out_specs=[VMEM] * len(shapes),
        scratch_shapes=[pltpu.VMEM(a.shape, a.dtype) for a in args]
        + [pltpu.SemaphoreType.DMA((3 + LOCAL,))],
        compiler_params=pltpu.CompilerParams(vmem_limit_bytes=60 * MIB),
    )(*args)


def shards(tokens, expert_ids, gate_scores, w_in, w_down):
    n_expert, n_tensor = lax.axis_size("expert"), lax.axis_size("tensor")
    groups = n_tensor // QUAD
    toks = tokens.shape[0]
    _, _, hid, _ = w_in.shape
    rows = n_expert * SLOTS
    ids, gates = expert_ids.T, gate_scores.T
    peers = [
        [e * n_tensor + QUAD * m + q for e in range(n_expert) for m in range(groups)]
        for q in range(QUAD)
    ]
    held = (n_expert, groups, SLOTS, LANES)

    def bf16(*shape):
        return jax.ShapeDtypeStruct(shape, jnp.bfloat16)

    def f32(*shape):
        return jax.ShapeDtypeStruct(shape, jnp.float32)

    def exchange(value, r):
        return lax.ppermute(value, "tensor", [(i, i ^ r) for i in range(n_tensor)])

    def deal(value):
        value = value.reshape(n_expert * groups, SLOTS, LANES)
        value = lax.all_to_all(
            value, ("expert", "tensor"), 0, 0, tiled=True, axis_index_groups=peers
        )
        return value.reshape(held)

    part = bf16(3 * LOCAL, hid, groups * LANES)
    sent, chip = start((ids, tokens, w_in, w_down), [bf16(*held), bf16(2, *part.shape)])
    chip, w_in, w_down = lax.optimization_barrier((exchange(chip, 2), w_in, w_down))
    keep, core = call(pack_kernel, [part, part], (w_in, w_down))
    core = exchange(core, 1)
    weights = (keep, core, chip, exchange(chip[1], 1))

    ids, gates, core = lax.optimization_barrier((ids, gates, core))
    top, slot_table = ids.shape[0], n_expert * TILE
    dense, spread, picking, shares = call(
        table_kernel,
        [
            bf16(rows, slot_table),
            bf16(slot_table, rows),
            bf16(top * toks, slot_table),
            f32(toks, top, LANES),
        ],
        (ids, gates),
    )
    pair = (2, 2 * hid, rows)
    x, send = call(
        up_kernel,
        [bf16(rows, groups * LANES), bf16(*pair)],
        (deal(sent), dense, weights[1], weights[3]),
    )
    got = exchange(send, 1)
    own = call(own_kernel, f32(*pair), (x, weights[0], weights[2]))
    half = bf16(2 * hid, rows)
    own, send0, send2 = call(add_kernel, [f32(*pair), half, half], (own, got))
    got0, got2 = exchange(send2, 2), exchange(send0, 2)
    hidden0 = call(functools.partial(act_kernel, 0), bf16(hid, rows), (own, got0))
    hidden1 = exchange(hidden0, 1)
    hidden2 = call(functools.partial(act_kernel, 1), bf16(hid, rows), (own, got2))
    hidden3 = exchange(hidden2, 1)
    hidden = (hidden0, hidden1, hidden2, hidden3)
    out = call(down_kernel, bf16(*held), (*hidden, spread, *weights))
    return call(combine_kernel, bf16(toks, LANES), (picking, shares, deal(out)))


def solution(mesh):
    in_specs = (
        P("expert", "tensor"),
        P("expert", None),
        P("expert", None),
        P("expert", None, "tensor", None),
        P("expert", "tensor", None),
    )
    out_specs = P("expert", "tensor")
    return jax.shard_map(shards, mesh=mesh, in_specs=in_specs, out_specs=out_specs, check_vma=False)
```

```python
import jax
import jax.numpy as jnp
from jax import lax
from jax.experimental import pallas as pl
from jax.experimental.pallas import tpu as pltpu
from jax.sharding import PartitionSpec as P

LANES = 128
CAPACITY = 3
QUAD = 4
LOCAL = 2
SLOTS = LOCAL * CAPACITY
STRIDE = 5
TILE = 8
VMEM = pl.BlockSpec(memory_space=pltpu.VMEM)
ANY = pl.BlockSpec(memory_space=pl.ANY)
MIB = 1024 * 1024


def iota(shape, dim):
    return lax.broadcasted_iota(jnp.int32, shape, dim)


def pair_column(values):
    top, toks = values.shape
    shape = (toks, top, toks)
    picked = jnp.where(iota(shape, 0) == iota(shape, 2), values[None], 0.0)
    return jnp.sum(picked, axis=2, keepdims=True)


def slot_rows(ids, owners):
    top, toks = ids.shape
    pairs = top * toks
    down = pair_column(ids.astype(jnp.float32)).reshape(pairs, 1)
    ip, iq = iota((pairs, pairs), 0), iota((pairs, pairs), 1)
    across = jnp.sum(jnp.where(ip == iq, down, 0.0), axis=0, keepdims=True)
    same = down == across
    slot_down = jnp.sum(jnp.where(same & (iq < ip), 1.0, 0.0), axis=1, keepdims=True)
    slot_across = jnp.sum(jnp.where(same & (ip < iq), 1.0, 0.0), axis=0, keepdims=True)

    def row(number, slot):
        number, slot = number.astype(jnp.int32), slot.astype(jnp.int32)
        place = number // LOCAL * STRIDE % owners
        return place * TILE + number % LOCAL * CAPACITY + slot

    return row(down, slot_down), row(across, slot_across)


def dense_row(shape, dim, owners):
    row = iota(shape, dim)
    slot = row % TILE
    return jnp.where(slot < SLOTS, slot * owners + row // TILE, -1)


def onehot(found):
    return jnp.where(found, 1.0, 0.0).astype(jnp.bfloat16)


def padded(values):
    owners = values.shape[0]
    blank = jnp.zeros((owners, TILE - SLOTS, LANES), values.dtype)
    return jnp.concatenate([values, blank], axis=1).reshape(owners * TILE, LANES)


def pack(w_in_ref, w_down_ref, out_ref, distance):
    place = lax.rem(lax.axis_index("tensor"), QUAD)
    for j in range(out_ref.shape[2] // LANES):
        owner = QUAD * j + jnp.bitwise_xor(place, distance)
        src = pl.ds(pl.multiple_of(owner * LANES, LANES), LANES)
        dst = pl.ds(j * LANES, LANES)
        for e in range(LOCAL):
            for g in range(2):
                out_ref[2 * e + g, :, dst] = w_in_ref[e, g, :, src]
            out_ref[2 * LOCAL + e, :, dst] = w_down_ref[e, :, src]


def start_kernel(
    ids_hbm, tok_hbm, w_in_hbm, w_down_hbm, sent_ref, chip_ref, ids_ref, tok_ref, w_in_ref, w_down_ref, sems
):
    moves = [(ids_hbm, ids_ref), (tok_hbm, tok_ref)]
    moves += [(w_in_hbm.at[e], w_in_ref.at[e]) for e in range(LOCAL)]
    moves += [(w_down_hbm, w_down_ref)]
    copies = [pltpu.make_async_copy(a, b, sems.at[i]) for i, (a, b) in enumerate(moves)]
    for copy in copies:
        copy.start()
    for copy in copies[:2]:
        copy.wait()

    owners, groups = sent_ref.shape[:2]
    toks = tok_ref.shape[0]
    _, across = slot_rows(ids_ref[...], owners)
    pairs = across.shape[1]
    token_of = onehot(iota((pairs, toks), 0) // (pairs // toks) == iota((pairs, toks), 1))
    values = jnp.dot(token_of, tok_ref[...], preferred_element_type=jnp.float32)
    placing = onehot(iota((owners * TILE, pairs), 0) == across)
    values = jnp.dot(placing, values.astype(jnp.bfloat16), preferred_element_type=jnp.float32)
    values = values.reshape(owners, TILE, LANES)[:, :SLOTS].astype(jnp.bfloat16)
    for m in range(groups):
        sent_ref[:, m] = values

    for copy in copies[2:]:
        copy.wait()
    pack(w_in_ref, w_down_ref, chip_ref.at[0], 2)
    pack(w_in_ref, w_down_ref, chip_ref.at[1], 3)


def pack_kernel(w_in_ref, w_down_ref, keep_ref, core_ref):
    pack(w_in_ref, w_down_ref, keep_ref, 0)
    pack(w_in_ref, w_down_ref, core_ref, 1)


def table_kernel(ids_ref, gates_ref, dense_ref, spread_ref, picking_ref, shares_ref):
    rows, held = dense_ref.shape
    owners = held // TILE
    dense_ref[...] = onehot(iota((rows, held), 0) == dense_row((1, held), 1, owners))
    spread_ref[...] = onehot(iota((held, rows), 1) == dense_row((held, 1), 0, owners))
    down, _ = slot_rows(ids_ref[...], owners)
    picking_ref[...] = onehot(down == iota(picking_ref.shape, 1))
    gates = gates_ref[...]
    shares = pair_column(gates / jnp.sum(gates, axis=0, keepdims=True))
    shares_ref[...] = jnp.broadcast_to(shares, shares_ref.shape)


def preact(w_ref, x):
    _, hid, depth = w_ref.shape
    rows = x.shape[0]
    both = lax.dot_general(
        w_ref[: 2 * LOCAL].reshape(2 * LOCAL * hid, depth),
        x,
        (((1,), (1,)), ((), ())),
        preferred_element_type=jnp.float32,
    )
    first = iota((2 * hid, rows), 1) < rows // LOCAL
    return jnp.where(first, both[: 2 * hid], both[2 * hid :])


def up_kernel(x_ref, dense_ref, w1_ref, w3_ref, dense_x_ref, send_ref):
    groups = x_ref.shape[1]
    x = jnp.concatenate(
        [padded(x_ref[:, m].astype(jnp.float32)).astype(jnp.bfloat16) for m in range(groups)],
        axis=1,
    )
    x = jnp.dot(dense_ref[...], x, preferred_element_type=jnp.float32).astype(jnp.bfloat16)
    dense_x_ref[...] = x
    send_ref[0] = preact(w1_ref, x).astype(jnp.bfloat16)
    send_ref[1] = preact(w3_ref, x).astype(jnp.bfloat16)


def own_kernel(x_ref, w0_ref, w2_ref, own_ref):
    x = x_ref[...]
    own_ref[0] = preact(w0_ref, x)
    own_ref[1] = preact(w2_ref.at[0], x)


def add_kernel(own_ref, got_ref, sum_ref, send_ref):
    total = own_ref[...] + got_ref[...].astype(jnp.float32)
    sum_ref[...] = total
    send_ref[...] = total.astype(jnp.bfloat16)


def act_kernel(own_ref, got_ref, out_ref):
    hid = out_ref.shape[1]
    for r in range(2):
        pre = own_ref[r] + got_ref[1 - r].astype(jnp.float32)
        gate, up = pre[:hid], pre[hid:]
        out_ref[r] = (gate / (1.0 + jnp.exp(-gate)) * up).astype(jnp.bfloat16)


def down_kernel(own_ref, got_ref, spread_ref, w0_ref, w1_ref, w2_ref, w3_ref, out_ref):
    owners, groups = out_ref.shape[:2]
    hid, rows = own_ref.shape[1:]
    first = iota((hid, rows), 1) < rows // LOCAL
    values, weights = [], []
    for r, w_ref in enumerate((w0_ref, w1_ref, w2_ref.at[0], w3_ref)):
        hidden = (got_ref if r % 2 else own_ref)[r // 2].astype(jnp.float32)
        values += [jnp.where(first, hidden, 0.0), jnp.where(first, 0.0, hidden)]
        weights.append(w_ref[2 * LOCAL :].reshape(LOCAL * hid, groups * LANES))
    values = jnp.concatenate(values, axis=0).astype(jnp.bfloat16)
    weights = jnp.concatenate(weights, axis=0)
    values = lax.dot_general(
        spread_ref[...], values, (((1,), (1,)), ((), ())), preferred_element_type=jnp.float32
    ).astype(jnp.bfloat16)
    out = jnp.dot(values, weights, preferred_element_type=jnp.float32)
    for m in range(groups):
        part = out[:, m * LANES : (m + 1) * LANES]
        out_ref[:, m] = part.reshape(owners, TILE, LANES)[:, :SLOTS].astype(jnp.bfloat16)


def combine_kernel(picking_ref, shares_ref, x_ref, out_ref):
    groups = x_ref.shape[1]
    values = x_ref[:, 0].astype(jnp.float32)
    for m in range(1, groups):
        values = values + x_ref[:, m].astype(jnp.float32)
    values = padded(values).astype(jnp.bfloat16)
    picked = jnp.dot(picking_ref[...], values, preferred_element_type=jnp.float32)
    mixed = jnp.sum(picked.reshape(shares_ref.shape) * shares_ref[...], axis=1)
    out_ref[...] = mixed.astype(jnp.bfloat16)


def call(kernel, shapes, args):
    return pl.pallas_call(
        kernel,
        out_shape=shapes,
        in_specs=[VMEM] * len(args),
        out_specs=jax.tree.map(lambda _: VMEM, shapes),
        compiler_params=pltpu.CompilerParams(vmem_limit_bytes=48 * MIB),
    )(*args)


def start(args, shapes):
    return pl.pallas_call(
        start_kernel,
        out_shape=shapes,
        in_specs=[ANY] * len(args),
        out_specs=[VMEM] * len(shapes),
        scratch_shapes=[pltpu.VMEM(a.shape, a.dtype) for a in args]
        + [pltpu.SemaphoreType.DMA((3 + LOCAL,))],
        compiler_params=pltpu.CompilerParams(vmem_limit_bytes=60 * MIB),
    )(*args)


def shards(tokens, expert_ids, gate_scores, w_in, w_down):
    n_expert, n_tensor = lax.axis_size("expert"), lax.axis_size("tensor")
    groups = n_tensor // QUAD
    toks = tokens.shape[0]
    _, _, hid, _ = w_in.shape
    rows = n_expert * SLOTS
    ids, gates = expert_ids.T, gate_scores.T
    order = sorted(range(n_expert), key=lambda e: e * STRIDE % n_expert)
    peers = [
        [e * n_tensor + QUAD * m + q for e in order for m in range(groups)]
        for q in range(QUAD)
    ]
    held = (n_expert, groups, SLOTS, LANES)

    def bf16(*shape):
        return jax.ShapeDtypeStruct(shape, jnp.bfloat16)

    def f32(*shape):
        return jax.ShapeDtypeStruct(shape, jnp.float32)

    def exchange(value, r):
        return lax.ppermute(value, "tensor", [(i, i ^ r) for i in range(n_tensor)])

    def deal(value):
        value = value.reshape(n_expert * groups, SLOTS, LANES)
        value = lax.all_to_all(
            value, ("expert", "tensor"), 0, 0, tiled=True, axis_index_groups=peers
        )
        return value.reshape(held)

    part = bf16(3 * LOCAL, hid, groups * LANES)
    sent, chip = start((ids, tokens, w_in, w_down), [bf16(*held), bf16(2, *part.shape)])
    chip, w_in, w_down = lax.optimization_barrier((exchange(chip, 2), w_in, w_down))
    keep, core = call(pack_kernel, [part, part], (w_in, w_down))
    core = exchange(core, 1)
    weights = (keep, core, chip, exchange(chip[1], 1))

    ids, gates, core = lax.optimization_barrier((ids, gates, core))
    top, slot_table = ids.shape[0], n_expert * TILE
    dense, spread, picking, shares = call(
        table_kernel,
        [
            bf16(rows, slot_table),
            bf16(slot_table, rows),
            bf16(top * toks, slot_table),
            f32(toks, top, LANES),
        ],
        (ids, gates),
    )
    pair = (2, 2 * hid, rows)
    x, send = call(
        up_kernel,
        [bf16(rows, groups * LANES), bf16(*pair)],
        (deal(sent), dense, weights[1], weights[3]),
    )
    got = exchange(send, 1)
    own = call(own_kernel, f32(*pair), (x, weights[0], weights[2]))
    own, send = call(add_kernel, [f32(*pair), bf16(*pair)], (own, got))
    hidden = call(act_kernel, bf16(2, hid, rows), (own, exchange(send, 2)))
    out = call(down_kernel, bf16(*held), (hidden, exchange(hidden, 1), spread, *weights))
    return call(combine_kernel, bf16(toks, LANES), (picking, shares, deal(out)))


def solution(mesh):
    in_specs = (
        P("expert", "tensor"),
        P("expert", None),
        P("expert", None),
        P("expert", None, "tensor", None),
        P("expert", "tensor", None),
    )
    out_specs = P("expert", "tensor")
    return jax.shard_map(shards, mesh=mesh, in_specs=in_specs, out_specs=out_specs, check_vma=False)
```

```python
import jax
import jax.numpy as jnp
from jax import lax
from jax.experimental import pallas as pl
from jax.experimental.pallas import tpu as pltpu
from jax.sharding import PartitionSpec as P

LANES = 128
CAPACITY = 3
QUAD = 4
LOCAL = 2
SLOTS = LOCAL * CAPACITY
TILE = 8
VMEM = pl.BlockSpec(memory_space=pltpu.VMEM)
ANY = pl.BlockSpec(memory_space=pl.ANY)
MIB = 1024 * 1024


def iota(shape, dim):
    return lax.broadcasted_iota(jnp.int32, shape, dim)


def pair_column(values):
    top, toks = values.shape
    shape = (toks, top, toks)
    picked = jnp.where(iota(shape, 0) == iota(shape, 2), values[None], 0.0)
    return jnp.sum(picked, axis=2, keepdims=True)


def slot_rows(ids):
    top, toks = ids.shape
    pairs = top * toks
    down = pair_column(ids.astype(jnp.float32)).reshape(pairs, 1)
    ip, iq = iota((pairs, pairs), 0), iota((pairs, pairs), 1)
    across = jnp.sum(jnp.where(ip == iq, down, 0.0), axis=0, keepdims=True)
    same = down == across
    slot_down = jnp.sum(jnp.where(same & (iq < ip), 1.0, 0.0), axis=1, keepdims=True)
    slot_across = jnp.sum(jnp.where(same & (ip < iq), 1.0, 0.0), axis=0, keepdims=True)

    def row(number, slot):
        number, slot = number.astype(jnp.int32), slot.astype(jnp.int32)
        return number // LOCAL * TILE + number % LOCAL * CAPACITY + slot

    return row(down, slot_down), row(across, slot_across)


def dense_row(shape, dim, owners):
    row = iota(shape, dim)
    slot = row % TILE
    return jnp.where(slot < SLOTS, slot * owners + row // TILE, -1)


def onehot(found):
    return jnp.where(found, 1.0, 0.0).astype(jnp.bfloat16)


def padded(values):
    owners = values.shape[0]
    blank = jnp.zeros((owners, TILE - SLOTS, LANES), values.dtype)
    return jnp.concatenate([values, blank], axis=1).reshape(owners * TILE, LANES)


def pack(w_in_ref, w_down_ref, out_ref, distance):
    place = lax.rem(lax.axis_index("tensor"), QUAD)
    for j in range(out_ref.shape[2] // LANES):
        owner = QUAD * j + jnp.bitwise_xor(place, distance)
        src = pl.ds(pl.multiple_of(owner * LANES, LANES), LANES)
        dst = pl.ds(j * LANES, LANES)
        for e in range(LOCAL):
            for g in range(2):
                out_ref[2 * e + g, :, dst] = w_in_ref[e, g, :, src]
            out_ref[2 * LOCAL + e, :, dst] = w_down_ref[e, :, src]


def start_kernel(
    ids_hbm, tok_hbm, w_in_hbm, w_down_hbm, sent_ref, chip_ref, ids_ref, tok_ref, w_in_ref, w_down_ref, sems
):
    moves = [(ids_hbm, ids_ref), (tok_hbm, tok_ref)]
    moves += [(w_in_hbm.at[e, g], w_in_ref.at[e, g]) for e in range(LOCAL) for g in range(2)]
    moves += [(w_down_hbm.at[e], w_down_ref.at[e]) for e in range(LOCAL)]
    copies = [pltpu.make_async_copy(a, b, sems.at[i]) for i, (a, b) in enumerate(moves)]
    for copy in copies:
        copy.start()
    for copy in copies[:2]:
        copy.wait()

    owners, groups = sent_ref.shape[:2]
    toks = tok_ref.shape[0]
    _, across = slot_rows(ids_ref[...])
    pairs = across.shape[1]
    token_of = onehot(iota((pairs, toks), 0) // (pairs // toks) == iota((pairs, toks), 1))
    values = jnp.dot(token_of, tok_ref[...], preferred_element_type=jnp.float32)
    placing = onehot(iota((owners * TILE, pairs), 0) == across)
    values = jnp.dot(placing, values.astype(jnp.bfloat16), preferred_element_type=jnp.float32)
    values = values.reshape(owners, TILE, LANES)[:, :SLOTS].astype(jnp.bfloat16)
    for m in range(groups):
        sent_ref[:, m] = values

    for copy in copies[2:]:
        copy.wait()
    pack(w_in_ref, w_down_ref, chip_ref.at[0], 2)
    pack(w_in_ref, w_down_ref, chip_ref.at[1], 3)


def pack_kernel(w_in_ref, w_down_ref, keep_ref, core_ref):
    pack(w_in_ref, w_down_ref, keep_ref, 0)
    pack(w_in_ref, w_down_ref, core_ref, 1)


def table_kernel(ids_ref, gates_ref, dense_ref, spread_ref, picking_ref, shares_ref):
    rows, held = dense_ref.shape
    owners = held // TILE
    dense_ref[...] = onehot(iota((rows, held), 0) == dense_row((1, held), 1, owners))
    spread_ref[...] = onehot(iota((held, rows), 1) == dense_row((held, 1), 0, owners))
    down, _ = slot_rows(ids_ref[...])
    picking_ref[...] = onehot(down == iota(picking_ref.shape, 1))
    gates = gates_ref[...]
    shares = pair_column(gates / jnp.sum(gates, axis=0, keepdims=True))
    shares_ref[...] = jnp.broadcast_to(shares, shares_ref.shape)


def preact(w_ref, x):
    _, hid, depth = w_ref.shape
    rows = x.shape[0]
    both = lax.dot_general(
        w_ref[: 2 * LOCAL].reshape(2 * LOCAL * hid, depth),
        x,
        (((1,), (1,)), ((), ())),
        preferred_element_type=jnp.float32,
    )
    first = iota((2 * hid, rows), 1) < rows // LOCAL
    return jnp.where(first, both[: 2 * hid], both[2 * hid :])


def up_kernel(x_ref, dense_ref, w1_ref, w3_ref, dense_x_ref, send_ref):
    groups = x_ref.shape[1]
    x = jnp.concatenate(
        [padded(x_ref[:, m].astype(jnp.float32)).astype(jnp.bfloat16) for m in range(groups)],
        axis=1,
    )
    x = jnp.dot(dense_ref[...], x, preferred_element_type=jnp.float32).astype(jnp.bfloat16)
    dense_x_ref[...] = x
    send_ref[0] = preact(w1_ref, x).astype(jnp.bfloat16)
    send_ref[1] = preact(w3_ref, x).astype(jnp.bfloat16)


def own_kernel(x_ref, w0_ref, w2_ref, own_ref):
    x = x_ref[...]
    own_ref[0] = preact(w0_ref, x)
    own_ref[1] = preact(w2_ref.at[0], x)


def add_kernel(own_ref, got_ref, sum_ref, send_ref):
    total = own_ref[...] + got_ref[...].astype(jnp.float32)
    sum_ref[...] = total
    send_ref[...] = total.astype(jnp.bfloat16)


def act_kernel(own_ref, got_ref, out_ref):
    hid = out_ref.shape[1]
    for r in range(2):
        pre = own_ref[r] + got_ref[1 - r].astype(jnp.float32)
        gate, up = pre[:hid], pre[hid:]
        out_ref[r] = (gate / (1.0 + jnp.exp(-gate)) * up).astype(jnp.bfloat16)


def down_kernel(own_ref, got_ref, spread_ref, w0_ref, w1_ref, w2_ref, w3_ref, out_ref):
    owners, groups = out_ref.shape[:2]
    hid, rows = own_ref.shape[1:]
    first = iota((hid, rows), 1) < rows // LOCAL
    values, weights = [], []
    for r, w_ref in enumerate((w0_ref, w1_ref, w2_ref.at[0], w3_ref)):
        hidden = (got_ref if r % 2 else own_ref)[r // 2].astype(jnp.float32)
        values += [jnp.where(first, hidden, 0.0), jnp.where(first, 0.0, hidden)]
        weights.append(w_ref[2 * LOCAL :].reshape(LOCAL * hid, groups * LANES))
    values = jnp.concatenate(values, axis=0).astype(jnp.bfloat16)
    weights = jnp.concatenate(weights, axis=0)
    values = lax.dot_general(
        spread_ref[...], values, (((1,), (1,)), ((), ())), preferred_element_type=jnp.float32
    ).astype(jnp.bfloat16)
    out = jnp.dot(values, weights, preferred_element_type=jnp.float32)
    for m in range(groups):
        part = out[:, m * LANES : (m + 1) * LANES]
        out_ref[:, m] = part.reshape(owners, TILE, LANES)[:, :SLOTS].astype(jnp.bfloat16)


def combine_kernel(picking_ref, shares_ref, x_ref, out_ref):
    groups = x_ref.shape[1]
    values = x_ref[:, 0].astype(jnp.float32)
    for m in range(1, groups):
        values = values + x_ref[:, m].astype(jnp.float32)
    values = padded(values).astype(jnp.bfloat16)
    picked = jnp.dot(picking_ref[...], values, preferred_element_type=jnp.float32)
    mixed = jnp.sum(picked.reshape(shares_ref.shape) * shares_ref[...], axis=1)
    out_ref[...] = mixed.astype(jnp.bfloat16)


def call(kernel, shapes, args):
    return pl.pallas_call(
        kernel,
        out_shape=shapes,
        in_specs=[VMEM] * len(args),
        out_specs=jax.tree.map(lambda _: VMEM, shapes),
        compiler_params=pltpu.CompilerParams(vmem_limit_bytes=48 * MIB),
    )(*args)


def start(args, shapes):
    return pl.pallas_call(
        start_kernel,
        out_shape=shapes,
        in_specs=[ANY] * len(args),
        out_specs=[VMEM] * len(shapes),
        scratch_shapes=[pltpu.VMEM(a.shape, a.dtype) for a in args]
        + [pltpu.SemaphoreType.DMA((2 + 3 * LOCAL,))],
        compiler_params=pltpu.CompilerParams(vmem_limit_bytes=60 * MIB),
    )(*args)


def shards(tokens, expert_ids, gate_scores, w_in, w_down):
    n_expert, n_tensor = lax.axis_size("expert"), lax.axis_size("tensor")
    groups = n_tensor // QUAD
    toks = tokens.shape[0]
    _, _, hid, _ = w_in.shape
    rows = n_expert * SLOTS
    ids, gates = expert_ids.T, gate_scores.T
    peers = [
        [e * n_tensor + QUAD * m + q for e in range(n_expert) for m in range(groups)]
        for q in range(QUAD)
    ]
    held = (n_expert, groups, SLOTS, LANES)

    def bf16(*shape):
        return jax.ShapeDtypeStruct(shape, jnp.bfloat16)

    def f32(*shape):
        return jax.ShapeDtypeStruct(shape, jnp.float32)

    def exchange(value, r):
        return lax.ppermute(value, "tensor", [(i, i ^ r) for i in range(n_tensor)])

    def deal(value):
        value = value.reshape(n_expert * groups, SLOTS, LANES)
        value = lax.all_to_all(
            value, ("expert", "tensor"), 0, 0, tiled=True, axis_index_groups=peers
        )
        return value.reshape(held)

    part = bf16(3 * LOCAL, hid, groups * LANES)
    sent, chip = start((ids, tokens, w_in, w_down), [bf16(*held), bf16(2, *part.shape)])
    chip, w_in, w_down = lax.optimization_barrier((exchange(chip, 2), w_in, w_down))
    keep, core = call(pack_kernel, [part, part], (w_in, w_down))
    core = exchange(core, 1)
    weights = (keep, core, chip, exchange(chip[1], 1))

    ids, gates, core = lax.optimization_barrier((ids, gates, core))
    top, slot_table = ids.shape[0], n_expert * TILE
    dense, spread, picking, shares = call(
        table_kernel,
        [
            bf16(rows, slot_table),
            bf16(slot_table, rows),
            bf16(top * toks, slot_table),
            f32(toks, top, LANES),
        ],
        (ids, gates),
    )
    pair = (2, 2 * hid, rows)
    x, send = call(
        up_kernel,
        [bf16(rows, groups * LANES), bf16(*pair)],
        (deal(sent), dense, weights[1], weights[3]),
    )
    got = exchange(send, 1)
    own = call(own_kernel, f32(*pair), (x, weights[0], weights[2]))
    own, send = call(add_kernel, [f32(*pair), bf16(*pair)], (own, got))
    hidden = call(act_kernel, bf16(2, hid, rows), (own, exchange(send, 2)))
    out = call(down_kernel, bf16(*held), (hidden, exchange(hidden, 1), spread, *weights))
    return call(combine_kernel, bf16(toks, LANES), (picking, shares, deal(out)))


def solution(mesh):
    in_specs = (
        P("expert", "tensor"),
        P("expert", None),
        P("expert", None),
        P("expert", None, "tensor", None),
        P("expert", "tensor", None),
    )
    out_specs = P("expert", "tensor")
    return jax.shard_map(shards, mesh=mesh, in_specs=in_specs, out_specs=out_specs, check_vma=False)
```
